32 devices in a mesh: ctx: 4 (over x, core), kv: 4 (over z), rep: 2 (over y).
Axes of the slice: x: 2, y: 2, z: 4, core: 2. Of those that a mesh axis runs over, the one named last changes fastest.
Arguments:
- queries: bfloat16 [2048, 8, 12, 128], P(('rep', 'ctx'), 'kv'), parts along dimension 0, may hold values from -100 to 100
- keys: bfloat16 [2048, 8, 128], P(('rep', 'ctx'), 'kv'), parts along dimension 0, may hold values from -4 to 4
- values: bfloat16 [2048, 8, 128], P(('rep', 'ctx'), 'kv'), parts along dimension 0, may hold values from -6 to 6
- output_gradient: bfloat16 [2048, 8, 12, 128], P(('rep', 'ctx'), 'kv'), parts along dimension 0, may hold values from -60 to 60
- band_start: int32 [2048], P(('rep', 'ctx')), parts along dimension 0, may hold values from 0 to 1023, as said below
Outputs:
- grad_query: float32 [2048, 8, 12, 128], P(('rep', 'ctx'), 'kv'), parts along dimension 0
- grad_key: float32 [2048, 8, 128], P(('rep', 'ctx'), 'kv'), parts along dimension 0
- grad_value: float32 [2048, 8, 128], P(('rep', 'ctx'), 'kv'), parts along dimension 0
The draws below stay inside these ranges and needn't reach their ends.
There are 2 independent parts, one for each index of `rep`. The reference program is written for one: setup_inputs(seed, part) draws one part's arguments, and reference() takes and returns one part's arrays. A program takes and returns all parts, laid end to end along the dimension named above; each array names one. Nothing has to cross between parts.
Inputs may be any that keep to these rules, and one draw needn't show every extreme that they name: For every row i, i - 2047 <= band_start[i] <= i and band_start[i] >= 0; the lower end i - 2047 is reached at some rows wherever i >= 2047.
All inputs are finite; a program needn't handle non-finite values.
Results may differ from the reference program's by a relative error of at most 0.003.
Values may be sent and summed in bfloat16 or wider, within the bound.
No kernel may reach another device: no remote copies, remote signals or barrier semaphores. Data moves between devices by JAX's collectives and lax.ppermute only.
A program may use at most 256 MiB of HBM per device.

```python
import jax
import jax.numpy as jnp
from jax import lax

KEY_VALUE_HEADS = 8
QUERY_PER_KEY = 12
HEAD_WIDTH = 128
TOK_DEV = 256
WINDOW = 2048
SEQUENCE_TOKENS = 1024


def paired_draw(key):
    base = jax.random.fold_in(key, 11)
    leading_key, following_key = jax.random.split(base, 2)
    sampled_keys = jnp.clip(jax.random.normal(following_key, (SEQUENCE_TOKENS, KEY_VALUE_HEADS, HEAD_WIDTH), jnp.float32), -4.0, 4.0)
    sampled_queries = jnp.clip(jax.random.normal(leading_key, (SEQUENCE_TOKENS, KEY_VALUE_HEADS, QUERY_PER_KEY, HEAD_WIDTH), jnp.float32), -4.0, 4.0)
    return (sampled_queries, sampled_keys)


def draw_queries(key, part):
    return paired_draw(key)[0].astype(jnp.bfloat16)


def draw_keys(key, part):
    return paired_draw(key)[1].astype(jnp.bfloat16)


def draw_band_start(key, part):
    base = jax.random.fold_in(key, 23)
    position = jnp.arange(SEQUENCE_TOKENS, dtype=jnp.int32)
    span_length = jax.random.randint(base, (SEQUENCE_TOKENS,), 1, WINDOW + 1)
    span_length = jnp.where(position % TOK_DEV == TOK_DEV - 1, WINDOW, span_length)
    return jnp.maximum(0, position - span_length + 1).astype(jnp.int32)


def levels(own_key, shape, pieces, low, high):
    loudness, own = 1.0, jax.random.fold_in(own_key, 6)
    for dim, shards_of in pieces:
        draws = jnp.exp(jax.random.uniform(jax.random.fold_in(own, dim), (shards_of,), jnp.float32, low / len(pieces), high / len(pieces)))
        loudness = loudness * jnp.repeat(draws, shape[dim] // shards_of).reshape([-1 if axis == dim else 1 for axis in range(len(shape))])
    return loudness


def bell_draw(own_key, dims, spread, most, pieces=(), kind=jnp.bfloat16):
    entries = jax.random.normal(own_key, dims, jnp.float32) * spread
    if len(pieces) > 0:
        entries = levels(own_key, dims, pieces, -0.22, 0.18) * entries
    return jnp.clip(entries, min=-most, max=most).astype(kind)


def setup_inputs(seed: int = 0, part: int = 0) -> dict:
    streams_of = jax.random.split(jax.random.key(seed), 6)
    part_splits = jax.random.split(jax.random.fold_in(streams_of[5], part), 6)
    queries = draw_queries(jax.random.fold_in(jax.random.fold_in(streams_of[5], part), 71), part)
    keys = draw_keys(jax.random.fold_in(jax.random.fold_in(streams_of[5], part), 71), part)
    values = bell_draw(part_splits[2], (SEQUENCE_TOKENS, KEY_VALUE_HEADS, HEAD_WIDTH), 1.0, 6.0, ((0, 4), (1, 4)))
    output_gradient = bell_draw(part_splits[3], (SEQUENCE_TOKENS, KEY_VALUE_HEADS, QUERY_PER_KEY, HEAD_WIDTH), 10.0, 60.0, ((0, 4), (1, 4)))
    band_start = draw_band_start(jax.random.fold_in(jax.random.fold_in(streams_of[5], part), 71), part)
    return dict(queries=queries, keys=keys, values=values, output_gradient=output_gradient, band_start=band_start)


def head_grads(query_head, key_head, value_head, cotangent_head, band_start):
    seq_len = query_head.shape[0]
    head_size = query_head.shape[2]
    scaling = head_size ** -0.5
    key_span = WINDOW + TOK_DEV
    padding = jnp.zeros((WINDOW, head_size), key_head.dtype)
    key_padded = jnp.concatenate([padding, key_head], 0)
    value_padded = jnp.concatenate([padding, value_head], 0)
    block_count = seq_len // TOK_DEV

    def one_block(carried, block_index):
        key_sum, value_sum = carried
        first_row = (block_index * TOK_DEV).astype(jnp.int32)
        query_block = lax.dynamic_slice_in_dim(query_head, first_row, TOK_DEV, 0).astype(jnp.float32)
        cotangent_block = lax.dynamic_slice_in_dim(cotangent_head, first_row, TOK_DEV, 0).astype(jnp.float32)
        key_block = lax.dynamic_slice_in_dim(key_padded, first_row, key_span, 0).astype(jnp.float32)
        value_block = lax.dynamic_slice_in_dim(value_padded, first_row, key_span, 0).astype(jnp.float32)
        start_block = lax.dynamic_slice_in_dim(band_start, first_row, TOK_DEV, 0)
        row_pos = first_row + jnp.arange(TOK_DEV, dtype=jnp.int32)
        key_pos = first_row - WINDOW + jnp.arange(key_span, dtype=jnp.int32)
        allowed = (key_pos[None, :] >= start_block[:, None]) & (key_pos[None, :] <= row_pos[:, None])
        allowed = allowed[:, None, :]
        scores = jnp.einsum('rgd,kd->rgk', query_block, key_block) * scaling
        grad_probs = jnp.einsum('rgd,kd->rgk', cotangent_block, value_block)
        row_max = jnp.max(jnp.where(allowed, scores, -1e30), -1)
        log_total = row_max + jnp.log(jnp.sum(jnp.where(allowed, jnp.exp(scores - row_max[..., None]), 0.0), -1))
        weights = jnp.where(allowed, jnp.exp(scores - log_total[..., None]), 0.0)
        dot_sum = jnp.sum(weights * grad_probs, -1)
        weights_bf = lax.optimization_barrier(weights.astype(jnp.bfloat16)).astype(jnp.float32)
        grad_scores = lax.optimization_barrier((weights * (grad_probs - dot_sum[..., None])).astype(jnp.bfloat16)).astype(jnp.float32)
        query_grad = jnp.einsum('rgk,kd->rgd', grad_scores, key_block) * scaling
        key_part = jnp.einsum('rgk,rgd->kd', grad_scores, query_block) * scaling
        value_part = jnp.einsum('rgk,rgd->kd', weights_bf, cotangent_block)
        old_keys = lax.dynamic_slice_in_dim(key_sum, first_row, key_span, 0)
        key_sum = lax.dynamic_update_slice_in_dim(key_sum, old_keys + key_part, first_row, 0)
        old_values = lax.dynamic_slice_in_dim(value_sum, first_row, key_span, 0)
        value_sum = lax.dynamic_update_slice_in_dim(value_sum, old_values + value_part, first_row, 0)
        return (key_sum, value_sum), query_grad

    zeros_init = jnp.zeros((seq_len + WINDOW, head_size), jnp.float32)
    (key_sum, value_sum), query_grads = lax.scan(one_block, (zeros_init, zeros_init), jnp.arange(block_count, dtype=jnp.int32))
    query_grads = query_grads.reshape(seq_len, query_head.shape[1], head_size)
    return query_grads, key_sum[WINDOW:], value_sum[WINDOW:]


def reference(queries, keys, values, output_gradient, band_start):
    def per_head(packed):
        return head_grads(packed[0], packed[1], packed[2], packed[3], band_start)

    stacked = (jnp.transpose(queries, (1, 0, 2, 3)), jnp.transpose(keys, (1, 0, 2)),
               jnp.transpose(values, (1, 0, 2)), jnp.transpose(output_gradient, (1, 0, 2, 3)))
    query_grads, key_grads, value_grads = lax.map(per_head, stacked)
    return (jnp.transpose(query_grads, (1, 0, 2, 3)), jnp.transpose(key_grads, (1, 0, 2)),
            jnp.transpose(value_grads, (1, 0, 2)))
```

```python
import functools

import jax
import jax.numpy as jnp
from jax import lax
from jax.experimental import pallas as pl
from jax.experimental.pallas import tpu as pltpu
from jax.sharding import PartitionSpec as P

WINDOW = 2048
LOG2E = 1.4426950408889634
MASKED = -1e30
f32 = jnp.float32
bf16 = jnp.bfloat16


def moved(block, distance):
    devices = range(lax.axis_size("ctx"))
    route = [(i - distance, i) for i in devices if i - distance in devices]
    return lax.ppermute(block, "ctx", route)


def swapped(block):
    return lax.ppermute(block, "ctx", [(i, i ^ 1) for i in range(lax.axis_size("ctx"))])


def attention_kernel(sizes, place_ref, q_ref, do_ref, start_ref, *refs):
    tokens, groups, heads, slots, width = sizes
    kv_refs = refs[:slots]
    dq_ref = refs[slots]
    part_refs = refs[slots + 1 : 2 * slots + 1]
    wide, q_s, do_s, k_s, v_s, bias, w_s, ds_s = refs[2 * slots + 1 :]
    keys = slots * tokens
    per_token = groups * heads
    scale = width**-0.5
    for source, split in ((q_ref, q_s), (do_ref, do_s)):
        wide[: tokens * per_token] = source[...].astype(f32)
        for h in range(heads):
            for g in range(groups):
                split[h, g * tokens : (g + 1) * tokens, :] = wide[
                    pl.ds(g * heads + h, tokens, stride=per_token), :
                ].astype(bf16)
    for slot in range(slots):
        for source, split in ((0, k_s), (1, v_s)):
            wide[: tokens * heads] = kv_refs[slot][source].astype(f32)
            for h in range(heads):
                split[h, slot * tokens : (slot + 1) * tokens, :] = wide[
                    pl.ds(h, tokens, stride=heads), :
                ].astype(bf16)
    row = place_ref[0] + lax.broadcasted_iota(jnp.int32, (tokens, 1), 0)
    for slot in range(slots):
        key = place_ref[1 + slot] + lax.broadcasted_iota(jnp.int32, (1, tokens), 1)
        bias[:, slot * tokens : (slot + 1) * tokens] = jnp.where(
            (key <= row) & (key >= start_ref[...]), 0.0, MASKED
        )
    across = (((1,), (1,)), ((), ()))
    down = (((0,), (0,)), ((), ()))
    for h in range(heads):

        def one_group(g, _):
            rows = pl.ds(pl.multiple_of(g * tokens, tokens), tokens)
            scores = lax.dot_general(q_s[h, rows, :], k_s[h], across, preferred_element_type=f32)
            probs = lax.dot_general(do_s[h, rows, :], v_s[h], across, preferred_element_type=f32)
            x = scores * (scale * LOG2E) + bias[...]
            p = jnp.exp2(x - jnp.max(x, -1, keepdims=True))
            inverse = 1.0 / jnp.sum(p, -1, keepdims=True)
            dot_sum = jnp.sum(p * probs, -1, keepdims=True) * inverse
            w = p * inverse
            w_s[rows, :] = w.astype(bf16)
            ds_s[rows, :] = (w * (probs - dot_sum)).astype(bf16)
            return 0

        lax.fori_loop(0, groups, one_group, 0, unroll=2)
        for g in range(0, groups, 2):
            dq = jnp.dot(
                ds_s[g * tokens : (g + 2) * tokens, :], k_s[h], preferred_element_type=f32
            )
            for k in range(2):
                dq_ref[pl.ds((g + k) * heads + h, tokens, stride=per_token), :] = (
                    dq[k * tokens : (k + 1) * tokens] * scale
                )
        dk = lax.dot_general(q_s[h], ds_s[...], down, preferred_element_type=f32) * scale
        dv = lax.dot_general(do_s[h], w_s[...], down, preferred_element_type=f32)
        for source, grad in ((0, dk), (1, dv)):
            turned = grad.T
            for slot in range(slots):
                wide[
                    pl.ds((source * slots + slot) * tokens * heads + h, tokens, stride=heads), :
                ] = turned[slot * tokens : (slot + 1) * tokens]
    for slot in range(slots):
        for source in range(2):
            first = (source * slots + slot) * tokens * heads
            part_refs[slot][source] = wide[first : first + tokens * heads].astype(
                part_refs[slot].dtype
            )


def attention(place, q, do, start, pairs, tokens, groups, heads):
    width = q.shape[-1]
    slots = len(pairs)
    rows = groups * tokens
    keys = slots * tokens
    vmem = pl.BlockSpec(memory_space=pltpu.VMEM)
    wide_rows = max(rows * heads, 2 * keys * heads)
    return pl.pallas_call(
        functools.partial(attention_kernel, (tokens, groups, heads, slots, width)),
        in_specs=[pl.BlockSpec(memory_space=pltpu.SMEM)] + [vmem] * (3 + slots),
        out_specs=[vmem] * (1 + slots),
        out_shape=[jax.ShapeDtypeStruct((rows * heads, width), f32)]
        + [
            jax.ShapeDtypeStruct((2, tokens * heads, width), f32 if slot == 0 else bf16)
            for slot in range(slots)
        ],
        scratch_shapes=[
            pltpu.VMEM((wide_rows, width), f32),
            pltpu.VMEM((heads, rows, width), bf16),
            pltpu.VMEM((heads, rows, width), bf16),
            pltpu.VMEM((heads, keys, width), bf16),
            pltpu.VMEM((heads, keys, width), bf16),
            pltpu.VMEM((tokens, keys), f32),
            pltpu.VMEM((rows, keys), bf16),
            pltpu.VMEM((rows, keys), bf16),
        ],
        compiler_params=pltpu.CompilerParams(vmem_limit_bytes=62 * 2**20),
    )(place, q, do, start, *pairs)


def shards(queries, keys, values, output_gradient, band_start):
    tokens, heads, groups, width = queries.shape
    ctx = lax.axis_index("ctx")
    count = lax.axis_size("ctx")
    reach = min(WINDOW // tokens, count - 1)
    hops = min((reach + 1) // 2, count // 2 - 1)
    own = jnp.stack([keys.reshape(tokens * heads, width), values.reshape(tokens * heads, width)], 0)
    same = [own] + [moved(own, 2 * d) for d in range(1, hops + 1)]
    other = [swapped(block) for block in same]
    partner = ctx + 1 - 2 * (ctx % 2)
    blocks = [ctx - 2 * d for d in range(hops + 1)] + [partner - 2 * d for d in range(hops + 1)]
    place = jnp.stack([ctx] + blocks).astype(jnp.int32) * tokens

    def flat(a):
        return a.transpose(0, 2, 1, 3).reshape(tokens * groups * heads, width)

    dq, *parts = attention(
        place,
        flat(queries),
        flat(output_gradient),
        band_start.reshape(tokens, 1),
        same + other,
        tokens,
        groups,
        heads,
    )
    back = [swapped(part) for part in parts[hops + 1 :]]
    total = parts[0] + back[0].astype(f32)
    for d in range(1, hops + 1):
        both = (parts[d].astype(f32) + back[d].astype(f32)).astype(bf16)
        total = total + moved(both, -2 * d).astype(f32)
    return (
        dq.reshape(tokens, groups, heads, width).transpose(0, 2, 1, 3),
        total[0].reshape(tokens, heads, width),
        total[1].reshape(tokens, heads, width),
    )


def solution(mesh):
    rows = P(("rep", "ctx"), "kv", None, None)
    keys = P(("rep", "ctx"), "kv", None)
    return jax.shard_map(
        shards,
        mesh=mesh,
        in_specs=(rows, keys, keys, rows, P(("rep", "ctx"))),
        out_specs=(rows, keys, keys),
        check_vma=False,
    )
```

```python
import functools

import jax
import jax.numpy as jnp
from jax import lax
from jax.experimental import pallas as pl
from jax.experimental.pallas import tpu as pltpu
from jax.sharding import PartitionSpec as P

WINDOW = 2048
LOG2E = 1.4426950408889634
MASKED = -1e30
f32 = jnp.float32
bf16 = jnp.bfloat16
ACROSS = (((1,), (1,)), ((), ()))
DOWN = (((0,), (0,)), ((), ()))
VMEM = pl.BlockSpec(memory_space=pltpu.VMEM)


def moved(block, distance):
    devices = range(lax.axis_size("ctx"))
    route = [(i - distance, i) for i in devices if i - distance in devices]
    return lax.ppermute(block, "ctx", route)


def swapped(block):
    return lax.ppermute(block, "ctx", [(i, i ^ 1) for i in range(lax.axis_size("ctx"))])


def split_heads(pair_refs, k_s, v_s, wide, tokens, heads):
    for slot, pair in enumerate(pair_refs):
        for source, split in ((0, k_s), (1, v_s)):
            wide[: tokens * heads] = pair[source].astype(f32)
            for h in range(heads):
                split[h, slot * tokens : (slot + 1) * tokens, :] = wide[
                    pl.ds(h, tokens, stride=heads), :
                ].astype(bf16)


def join_heads(dk, dv, part_refs, wide, tokens, heads, scale):
    for source, grad in ((0, dk), (1, dv)):
        for slot, part in enumerate(part_refs):
            for h in range(heads):
                block = grad[h, :, slot * tokens : (slot + 1) * tokens].T
                wide[pl.ds(h, tokens, stride=heads), :] = block * scale if source == 0 else block
            part[source] = wide[: tokens * heads].astype(part.dtype)


def fill_bias(bias, start_ref, first_keys, tokens):
    down = lax.broadcasted_iota(jnp.int32, (tokens, tokens), 0)
    along = lax.broadcasted_iota(jnp.int32, (tokens, tokens), 1)
    start = jnp.sum(
        jnp.where(down == along, start_ref[...].astype(f32), 0.0), -1, keepdims=True
    ).astype(jnp.int32)
    row = lax.axis_index("ctx") * tokens + lax.broadcasted_iota(jnp.int32, (tokens, 1), 0)
    for slot, first in enumerate(first_keys):
        key = first + lax.broadcasted_iota(jnp.int32, (1, tokens), 1)
        bias[:, slot * tokens : (slot + 1) * tokens] = jnp.where(
            (key <= row) & (key >= start), 0.0, MASKED
        )


def take(table, column):
    lane = lax.broadcasted_iota(jnp.int32, table.shape, 1)
    return jnp.sum(jnp.where(lane == column, table[...], 0.0), -1, keepdims=True)


def put(table, column, value):
    lane = lax.broadcasted_iota(jnp.int32, table.shape, 1)
    table[...] = jnp.where(lane == column, value, table[...])


def near_kernel(
    sizes, q_ref, do_ref, start_ref, own_ref, partner_ref,
    qs_ref, dos_ref, w_ref, u_ref, k_ref, log_ref, dot_ref,
    wide, v_s, bias, s_a, d_a, s_b, d_b, *copies,
):
    tokens, groups, heads, width, per, kept = sizes
    chunk = per * tokens
    chunks = groups // per * heads
    i = pl.program_id(0)
    first = step_rows(kept, 2 * chunk)
    slope = width**-0.5 * LOG2E
    qs, dos = (qs_ref, dos_ref) if kept else copies

    def products(c, s, d):
        rows = pl.ds(pl.multiple_of(c * chunk, chunk), chunk)
        h = c * per // groups
        s[...] = lax.dot_general(qs[rows, :], k_ref[h], ACROSS, preferred_element_type=f32)
        d[...] = lax.dot_general(dos[rows, :], v_s[h], ACROSS, preferred_element_type=f32)

    def weights(c, half, s, d):
        for g in range(per):
            rows = slice(g * tokens, (g + 1) * tokens)
            out = pl.ds(first + half * chunk + g * tokens, tokens)
            x = s[rows, :] * slope + bias[...]
            dp = d[rows, :]
            m = jnp.max(x, -1, keepdims=True)
            p = jnp.exp2(x - m)
            total = jnp.sum(p, -1, keepdims=True)
            inverse = 1.0 / total
            dot = jnp.sum(p * dp, -1, keepdims=True) * inverse
            w = p * inverse
            w_ref[out, :] = w.astype(bf16)
            u_ref[out, :] = (w * (dp - dot)).astype(bf16)
            put(log_ref, c * per + g, m + jnp.log2(total))
            put(dot_ref, c * per + g, dot)

    @pl.when(i == 0)
    def _():
        for source, split in ((q_ref, qs), (do_ref, dos)):
            wide[...] = source[...].astype(f32)
            for h in range(heads):
                for g in range(groups):
                    at = (h * groups + g) * tokens
                    split[at : at + tokens, :] = wide[
                        pl.ds(g * heads + h, tokens, stride=groups * heads), :
                    ].astype(bf16)
        split_heads((own_ref, partner_ref), k_ref, v_s, wide, tokens, heads)
        ctx = lax.axis_index("ctx")
        fill_bias(bias, start_ref, (ctx * tokens, (ctx + 1 - 2 * (ctx % 2)) * tokens), tokens)
        log_ref[...] = jnp.zeros_like(log_ref)
        dot_ref[...] = jnp.zeros_like(dot_ref)
        products(0, s_a, d_a)

    if not kept:
        both = pl.ds(pl.multiple_of(i * 2 * chunk, 2 * chunk), 2 * chunk)
        qs_ref[...] = qs[both, :]
        dos_ref[...] = dos[both, :]
    products(2 * i + 1, s_b, d_b)
    weights(2 * i, 0, s_a, d_a)
    products(jnp.minimum(2 * i + 2, chunks - 1), s_a, d_a)
    weights(2 * i + 1, 1, s_b, d_b)


def far_kernel(
    sizes, start_ref, log1_ref, dot1_ref, qs_ref, dos_ref, *refs,
):
    tokens, groups, heads, slots, width, per, kept = sizes
    pair_refs = refs[:slots]
    k_ref, ds_ref, log_ref, dot_ref = refs[slots : slots + 4]
    part_refs = refs[slots + 4 : 2 * slots + 4]
    wide, v_s, bias, w_s, dk, dv, s_a, d_a, s_b, d_b = refs[2 * slots + 4 :]
    chunk = per * tokens
    chunks = groups // per * heads
    hops = slots // 2
    i = pl.program_id(0)
    first = step_rows(kept, 2 * chunk)
    slope = width**-0.5 * LOG2E

    def products(c, s, d):
        rows = pl.ds(pl.multiple_of(c * chunk, chunk), chunk)
        h = c * per // groups
        s[...] = lax.dot_general(qs_ref[rows, :], k_ref[h], ACROSS, preferred_element_type=f32)
        d[...] = lax.dot_general(dos_ref[rows, :], v_s[h], ACROSS, preferred_element_type=f32)

    def weights(c, half, s, d):
        for g in range(per):
            rows = slice(g * tokens, (g + 1) * tokens)
            out = pl.ds(first + half * chunk + g * tokens, tokens)
            log1 = take(log1_ref, c * per + g)
            dot1 = take(dot1_ref, c * per + g)
            x = s[rows, :] * slope + bias[...]
            dp = d[rows, :]
            m = jnp.maximum(jnp.max(x, -1, keepdims=True), log1)
            p = jnp.exp2(x - m)
            before = jnp.exp2(log1 - m)
            total = jnp.sum(p, -1, keepdims=True) + before
            inverse = 1.0 / total
            dot = (jnp.sum(p * dp, -1, keepdims=True) + before * dot1) * inverse
            w = p * inverse
            w_s[half * chunk + g * tokens : half * chunk + (g + 1) * tokens, :] = w.astype(bf16)
            ds_ref[out, :] = (w * (dp - dot)).astype(bf16)
            put(log_ref, c * per + g, m + jnp.log2(total))
            put(dot_ref, c * per + g, dot)

    @pl.when(i == 0)
    def _():
        split_heads(pair_refs, k_ref, v_s, wide, tokens, heads)
        ctx = lax.axis_index("ctx")
        partner = ctx + 1 - 2 * (ctx % 2)
        starts = [(ctx - 2 * d) * tokens for d in range(1, hops + 1)]
        starts += [(partner - 2 * d) * tokens for d in range(1, hops + 1)]
        fill_bias(bias, start_ref, starts, tokens)
        log_ref[...] = jnp.zeros_like(log_ref)
        dot_ref[...] = jnp.zeros_like(dot_ref)
        dk[...] = jnp.zeros_like(dk)
        dv[...] = jnp.zeros_like(dv)
        products(0, s_a, d_a)

    products(2 * i + 1, s_b, d_b)
    weights(2 * i, 0, s_a, d_a)
    products(jnp.minimum(2 * i + 2, chunks - 1), s_a, d_a)
    weights(2 * i + 1, 1, s_b, d_b)
    both = pl.ds(pl.multiple_of(i * 2 * chunk, 2 * chunk), 2 * chunk)
    h = i * 2 * per // groups
    these = pl.ds(first, 2 * chunk)
    dk[h] += lax.dot_general(qs_ref[both, :], ds_ref[these, :], DOWN, preferred_element_type=f32)
    dv[h] += lax.dot_general(dos_ref[both, :], w_s[...], DOWN, preferred_element_type=f32)

    @pl.when(i == pl.num_programs(0) - 1)
    def _():
        join_heads(dk, dv, part_refs, wide, tokens, heads, width**-0.5)


def tail_kernel(
    sizes, log1_ref, dot1_ref, log_ref, dot_ref, k1_ref, k2_ref, qs_ref, dos_ref, w1_ref, u1_ref, ds2_ref,
    dq_ref, own_ref, partner_ref,
    wide, w_s, ds_s, dk, dv,
):
    tokens, groups, heads, width, per, kept = sizes
    chunk = per * tokens
    i = pl.program_id(0)
    scale = width**-0.5
    h = i * 2 * per // groups
    first = step_rows(kept, 2 * chunk)
    these = pl.ds(first, 2 * chunk)

    @pl.when(i == 0)
    def _():
        dk[...] = jnp.zeros_like(dk)
        dv[...] = jnp.zeros_like(dv)

    for g in range(2 * per):
        rows = slice(g * tokens, (g + 1) * tokens)
        column = i * 2 * per + g
        share = jnp.exp2(take(log1_ref, column) - take(log_ref, column))
        shift = take(dot1_ref, column) - take(dot_ref, column)
        here = pl.ds(first + g * tokens, tokens)
        w = w1_ref[here, :].astype(f32)
        w_s[rows, :] = (w * share).astype(bf16)
        ds_s[rows, :] = ((u1_ref[here, :].astype(f32) + w * shift) * share).astype(bf16)
    dk[h] += lax.dot_general(qs_ref[these, :], ds_s[...], DOWN, preferred_element_type=f32)
    dv[h] += lax.dot_general(dos_ref[these, :], w_s[...], DOWN, preferred_element_type=f32)
    dq = jnp.dot(ds_s[...], k1_ref[h], preferred_element_type=f32)
    dq += jnp.dot(ds2_ref[these, :], k2_ref[h], preferred_element_type=f32)
    dq *= scale
    group = i * 2 * per % groups
    for g in range(2 * per):
        dq_ref[pl.ds((group + g) * heads + h, tokens, stride=groups * heads), :] = dq[
            g * tokens : (g + 1) * tokens
        ]

    @pl.when(i == pl.num_programs(0) - 1)
    def _():
        join_heads(dk, dv, (own_ref, partner_ref), wide, tokens, heads, scale)


def whole(*shape):
    return pl.BlockSpec(shape, lambda i: (0,) * len(shape))


def stepped(kept, *shape):
    return VMEM if kept else pl.BlockSpec(shape, lambda i: (i, 0))


def params(kept):
    return pltpu.CompilerParams(vmem_limit_bytes=(24 if kept else 60) * 2**20)


def step_rows(kept, rows):
    if not kept:
        return 0
    return pl.multiple_of(pl.program_id(0) * rows, rows)


def near(q, do, start, own, partner, sizes):
    tokens, groups, heads, width, per, kept = sizes
    chunk = per * tokens
    rows = tokens * groups * heads
    keys = 2 * tokens
    return pl.pallas_call(
        functools.partial(near_kernel, sizes),
        grid=(rows // (2 * chunk),),
        in_specs=[VMEM] * 5,
        out_specs=[
            stepped(kept, 2 * chunk, width),
            stepped(kept, 2 * chunk, width),
            stepped(kept, 2 * chunk, keys),
            stepped(kept, 2 * chunk, keys),
            whole(heads, keys, width),
            whole(tokens, 128),
            whole(tokens, 128),
        ],
        out_shape=[
            jax.ShapeDtypeStruct((rows, width), bf16),
            jax.ShapeDtypeStruct((rows, width), bf16),
            jax.ShapeDtypeStruct((rows, keys), bf16),
            jax.ShapeDtypeStruct((rows, keys), bf16),
            jax.ShapeDtypeStruct((heads, keys, width), bf16),
            jax.ShapeDtypeStruct((tokens, 128), f32),
            jax.ShapeDtypeStruct((tokens, 128), f32),
        ],
        scratch_shapes=[
            pltpu.VMEM((rows, width), f32),
            pltpu.VMEM((heads, keys, width), bf16),
            pltpu.VMEM((tokens, keys), f32),
        ]
        + [pltpu.VMEM((chunk, keys), f32)] * 4
        + [pltpu.VMEM((rows, width), bf16)] * (0 if kept else 2),
        compiler_params=params(kept),
        cost_estimate=pl.CostEstimate(
            flops=2 * 2 * rows * (keys) * width,
            bytes_accessed=8 * rows * (keys),
            transcendentals=rows * (keys),
        ),
        name="near",
    )(q, do, start, own, partner)


def far(start, log1, dot1, qs, dos, pairs, sizes):
    tokens, groups, heads, width, per, kept = sizes
    slots = len(pairs)
    chunk = per * tokens
    rows = tokens * groups * heads
    keys = slots * tokens
    return pl.pallas_call(
        functools.partial(far_kernel, (tokens, groups, heads, slots, width, per, kept)),
        grid=(rows // (2 * chunk),),
        in_specs=[VMEM] * (5 + slots),
        out_specs=[
            whole(heads, keys, width),
            stepped(kept, 2 * chunk, keys),
            whole(tokens, 128),
            whole(tokens, 128),
        ]
        + [whole(2, tokens * heads, width)] * slots,
        out_shape=[
            jax.ShapeDtypeStruct((heads, keys, width), bf16),
            jax.ShapeDtypeStruct((rows, keys), bf16),
            jax.ShapeDtypeStruct((tokens, 128), f32),
            jax.ShapeDtypeStruct((tokens, 128), f32),
        ]
        + [jax.ShapeDtypeStruct((2, tokens * heads, width), bf16)] * slots,
        scratch_shapes=[
            pltpu.VMEM((tokens * heads, width), f32),
            pltpu.VMEM((heads, keys, width), bf16),
            pltpu.VMEM((tokens, keys), f32),
            pltpu.VMEM((2 * chunk, keys), bf16),
            pltpu.VMEM((heads, width, keys), f32),
            pltpu.VMEM((heads, width, keys), f32),
        ]
        + [pltpu.VMEM((chunk, keys), f32)] * 4,
        compiler_params=params(kept),
        cost_estimate=pl.CostEstimate(
            flops=2 * 4 * rows * (keys) * width,
            bytes_accessed=8 * rows * (keys),
            transcendentals=rows * (keys),
        ),
        name="far",
    )(start, log1, dot1, qs, dos, *pairs)


def tail(log1, dot1, log, dot, k1, k2, qs, dos, w1, u1, ds2, sizes):
    tokens, groups, heads, width, per, kept = sizes
    chunk = per * tokens
    rows = tokens * groups * heads
    near_keys, far_keys = k1.shape[1], k2.shape[1]
    return pl.pallas_call(
        functools.partial(tail_kernel, sizes),
        grid=(rows // (2 * chunk),),
        in_specs=[whole(tokens, 128)] * 4
        + [
            whole(heads, near_keys, width),
            whole(heads, far_keys, width),
            stepped(kept, 2 * chunk, width),
            stepped(kept, 2 * chunk, width),
            stepped(kept, 2 * chunk, near_keys),
            stepped(kept, 2 * chunk, near_keys),
            stepped(kept, 2 * chunk, far_keys),
        ],
        out_specs=[VMEM] * 3,
        out_shape=[
            jax.ShapeDtypeStruct((rows, width), f32),
            jax.ShapeDtypeStruct((2, tokens * heads, width), f32),
            jax.ShapeDtypeStruct((2, tokens * heads, width), bf16),
        ],
        scratch_shapes=[
            pltpu.VMEM((tokens * heads, width), f32),
            pltpu.VMEM((2 * chunk, near_keys), bf16),
            pltpu.VMEM((2 * chunk, near_keys), bf16),
            pltpu.VMEM((heads, width, near_keys), f32),
            pltpu.VMEM((heads, width, near_keys), f32),
        ],
        compiler_params=params(kept),
        cost_estimate=pl.CostEstimate(
            flops=2 * 3 * rows * (near_keys + far_keys) * width,
            bytes_accessed=8 * rows * (near_keys + far_keys),
            transcendentals=rows * (near_keys + far_keys),
        ),
        name="tail",
    )(log1, dot1, log, dot, k1, k2, qs, dos, w1, u1, ds2)


def shards(queries, keys, values, output_gradient, band_start):
    tokens, heads, groups, width = queries.shape
    count = lax.axis_size("ctx")
    reach = min(WINDOW // tokens, count - 1)
    hops = min((reach + 1) // 2, count // 2 - 1)
    own = jnp.stack([keys.reshape(tokens * heads, width), values.reshape(tokens * heads, width)], 0)
    same = [moved(own, 2 * d) for d in range(1, hops + 1)]
    partner = swapped(own)
    start = band_start.reshape(1, tokens)
    per = next(n for n in (3, 2, 1) if groups % (2 * n) == 0 and n * hops <= 4)
    kept = hops <= 2
    sizes = (tokens, groups, heads, width, per, kept)

    def flat(a):
        return a.transpose(0, 2, 1, 3).reshape(tokens * groups * heads, width)

    qs, dos, w1, u1, k1, log1, dot1 = near(
        flat(queries), flat(output_gradient), start, own, partner, sizes
    )
    *same, log1 = lax.optimization_barrier((*same, log1))
    other = [swapped(block) for block in same]
    k2, ds2, log, dot, *parts = far(start, log1, dot1, qs, dos, same + other, sizes)
    arriving = []
    for d in range(hops):
        crossed = swapped(parts[hops + d])
        both = (parts[d].astype(f32) + crossed.astype(f32)).astype(bf16)
        both, log = lax.optimization_barrier((both, log))
        arriving.append(moved(both, -2 * (d + 1)))
    dq, total, crossing = tail(log1, dot1, log, dot, k1, k2, qs, dos, w1, u1, ds2, sizes)
    crossing, *arriving = lax.optimization_barrier((crossing, *arriving))
    total = total + swapped(crossing).astype(f32)
    for part in arriving:
        total = total + part.astype(f32)
    return (
        dq.reshape(tokens, groups, heads, width).transpose(0, 2, 1, 3),
        total[0].reshape(tokens, heads, width),
        total[1].reshape(tokens, heads, width),
    )


def solution(mesh):
    rows = P(("rep", "ctx"), "kv", None, None)
    keys = P(("rep", "ctx"), "kv", None)
    return jax.shard_map(
        shards,
        mesh=mesh,
        in_specs=(rows, keys, keys, rows, P(("rep", "ctx"))),
        out_specs=(rows, keys, keys),
        check_vma=False,
    )
```

```python
import functools

import jax
import jax.numpy as jnp
from jax import lax
from jax.experimental import pallas as pl
from jax.experimental.pallas import tpu as pltpu
from jax.sharding import PartitionSpec as P

WINDOW = 2048
LOG2E = 1.4426950408889634
MASKED = -1e30
f32 = jnp.float32
bf16 = jnp.bfloat16
ACROSS = (((1,), (1,)), ((), ()))
VMEM = pl.BlockSpec(memory_space=pltpu.VMEM)


def moved(block, distance):
    devices = range(lax.axis_size("ctx"))
    route = [(i - distance, i) for i in devices if i - distance in devices]
    return lax.ppermute(block, "ctx", route)


def swapped(block):
    return lax.ppermute(block, "ctx", [(i, i ^ 1) for i in range(lax.axis_size("ctx"))])


def split_heads(pair_refs, k_s, v_s, wide, tokens, heads):
    for slot, pair in enumerate(pair_refs):
        for source, split in ((0, k_s), (1, v_s)):
            wide[: tokens * heads] = pair[source].astype(f32)
            for h in range(heads):
                split[h, slot * tokens : (slot + 1) * tokens, :] = wide[
                    pl.ds(h, tokens, stride=heads), :
                ].astype(bf16)


def join_heads(dk, dv, part_refs, wide, tokens, heads, scale):
    for source, grad in ((0, dk), (1, dv)):
        for slot, part in enumerate(part_refs):
            for h in range(heads):
                block = grad[h, :, slot * tokens : (slot + 1) * tokens].T
                wide[pl.ds(h, tokens, stride=heads), :] = block * scale if source == 0 else block
            part[source] = wide[: tokens * heads].astype(part.dtype)


def fill_bias(bias, start_ref, first_keys, tokens):
    down = lax.broadcasted_iota(jnp.int32, (tokens, tokens), 0)
    along = lax.broadcasted_iota(jnp.int32, (tokens, tokens), 1)
    start = jnp.sum(
        jnp.where(down == along, start_ref[...].astype(f32), 0.0), -1, keepdims=True
    ).astype(jnp.int32)
    row = lax.axis_index("ctx") * tokens + lax.broadcasted_iota(jnp.int32, (tokens, 1), 0)
    for slot, first in enumerate(first_keys):
        key = first + lax.broadcasted_iota(jnp.int32, (1, tokens), 1)
        bias[:, slot * tokens : (slot + 1) * tokens] = jnp.where(
            (key <= row) & (key >= start), 0.0, MASKED
        )


def spread(lanes, width):
    return jnp.concatenate([lanes] * (width // lanes.shape[1]), 1)


def prep_kernel(sizes, q_ref, do_ref, qs_ref, dos_ref, wide, q_in, do_in, arrived):
    tokens, groups, heads, width, per, kept = sizes
    pieces = q_in.shape[0]
    here = tokens // pieces
    size = here * groups * heads
    loads = []
    for n in range(pieces):
        for k, (source, target) in enumerate(((q_ref, q_in), (do_ref, do_in))):
            load = pltpu.make_async_copy(
                source.at[pl.ds(n * size, size), :], target.at[n], arrived.at[n, k]
            )
            load.start()
            loads.append(load)
    for n in range(pieces):
        for k, (source, split) in enumerate(((q_in, qs_ref), (do_in, dos_ref))):
            loads[2 * n + k].wait()
            wide[2 * n + k] = source[n].astype(f32)
            for h in range(heads):
                for g in range(groups):
                    at = (h * groups + g) * tokens + n * here
                    split[at : at + here, :] = wide[
                        2 * n + k, pl.ds(g * heads + h, here, stride=groups * heads), :
                    ].astype(bf16)


def near_kernel(
    sizes, qs, dos, start_ref, own_ref, partner_ref,
    w_ref, u_ref, k_ref, log_ref, mean_ref, qt_ref, dot_ref,
    wide, v_s, bias, s_a, d_a, s_b, d_b,
):
    tokens, groups, heads, width, per, kept = sizes
    chunk = per * tokens
    chunks = groups // per * heads
    i = pl.program_id(0)
    first = step_rows(kept, 2 * chunk)
    slope = width**-0.5 * LOG2E

    def products(c, s, d):
        rows = pl.ds(pl.multiple_of(c * chunk, chunk), chunk)
        h = c * per // groups
        s[...] = lax.dot_general(qs[rows, :], k_ref[h], ACROSS, preferred_element_type=f32)
        d[...] = lax.dot_general(dos[rows, :], v_s[h], ACROSS, preferred_element_type=f32)

    def weights(c, half, s, d):
        for g in range(per):
            rows = slice(g * tokens, (g + 1) * tokens)
            out = pl.ds(first + half * chunk + g * tokens, tokens)
            x = s[rows, :] * slope + bias[...]
            dp = d[rows, :]
            m = jnp.max(x, -1, keepdims=True)
            p = jnp.exp2(x - m)
            total = jnp.sum(p, -1, keepdims=True)
            inverse = 1.0 / total
            dot = jnp.sum(p * dp, -1, keepdims=True) * inverse
            w = p * inverse
            w_ref[out, :] = w.astype(bf16)
            u_ref[out, :] = (w * (dp - dot)).astype(bf16)
            log_ref[out, :] = jnp.broadcast_to(m + jnp.log2(total), (tokens, 128))
            mean_ref[out, :] = jnp.broadcast_to(dot, (tokens, 128))

    @pl.when(i == 0)
    def _():
        split_heads((own_ref, partner_ref), k_ref, v_s, wide, tokens, heads)
        ctx = lax.axis_index("ctx")
        fill_bias(bias, start_ref, (ctx * tokens, (ctx + 1 - 2 * (ctx % 2)) * tokens), tokens)
        products(0, s_a, d_a)

    both = pl.ds(pl.multiple_of(i * 2 * chunk, 2 * chunk), 2 * chunk)
    columns = pl.ds(first, 2 * chunk)
    products(2 * i + 1, s_b, d_b)
    qt_ref[:, columns] = qs[both, :].T
    weights(2 * i, 0, s_a, d_a)
    products(jnp.minimum(2 * i + 2, chunks - 1), s_a, d_a)
    dot_ref[:, columns] = dos[both, :].T
    weights(2 * i + 1, 1, s_b, d_b)


def far_kernel(
    sizes, start_ref, log1_ref, mean1_ref, qs_ref, dos_ref, qt_ref, dot_ref, *refs,
):
    tokens, groups, heads, slots, width, per, kept = sizes
    pair_refs = refs[:slots]
    k_ref, ds_ref, share_ref, shift_ref = refs[slots : slots + 4]
    part_refs = refs[slots + 4 : 2 * slots + 4]
    wide, v_s, bias, dk, dv, s_a, d_a, s_b, d_b, w_s, *ds_s = refs[2 * slots + 4 :]
    chunk = per * tokens
    chunks = groups // per * heads
    hops = slots // 2
    i = pl.program_id(0)
    first = step_rows(kept, 2 * chunk)
    slope = width**-0.5 * LOG2E
    ctx = lax.axis_index("ctx")
    reached = ctx >= 2
    steps = groups // (2 * per)
    inside = pl.multiple_of(i % steps * 2 * chunk, 2 * chunk)

    def products(c, s, d):
        rows = pl.ds(pl.multiple_of(c * chunk, chunk), chunk)
        h = c * per // groups
        s[...] = lax.dot_general(qs_ref[rows, :], k_ref[h], ACROSS, preferred_element_type=f32)
        d[...] = lax.dot_general(dos_ref[rows, :], v_s[h], ACROSS, preferred_element_type=f32)

    def gradients():
        h = i // steps
        rows = pl.ds(pl.multiple_of(h * groups * tokens, groups * tokens), groups * tokens)
        ds = ds_ref[rows, :] if kept else ds_s[0][...]
        dk[h] = jnp.dot(qt_ref[:, rows], ds, preferred_element_type=f32)
        dv[h] = jnp.dot(dot_ref[:, rows], w_s[...], preferred_element_type=f32)

    def weights(c, half, s, d):
        for g in range(per):
            rows = slice(g * tokens, (g + 1) * tokens)
            out = pl.ds(first + half * chunk + g * tokens, tokens)
            log1 = log1_ref[out, :]
            mean1 = mean1_ref[out, :]
            x = s[rows, :] * slope + bias[...]
            dp = d[rows, :]
            m = jnp.maximum(jnp.max(x, -1, keepdims=True), log1)
            p = jnp.exp2(x - spread(m, x.shape[1]))
            before = jnp.exp2(log1 - m)
            inverse = 1.0 / (jnp.sum(p, -1, keepdims=True) + before)
            mean = (jnp.sum(p * dp, -1, keepdims=True) + before * mean1) * inverse
            w = p * spread(inverse, x.shape[1])
            ds = (w * (dp - spread(mean, x.shape[1]))).astype(bf16)
            here = pl.ds(inside + half * chunk + g * tokens, tokens)
            w_s[here, :] = w.astype(bf16)
            ds_ref[out, :] = ds
            if not kept:
                ds_s[0][here, :] = ds
            share_ref[out, :] = before * inverse
            shift_ref[out, :] = mean1 - mean

    @pl.when(reached & (i == 0))
    def _():
        split_heads(pair_refs, k_ref, v_s, wide, tokens, heads)
        partner = ctx + 1 - 2 * (ctx % 2)
        starts = [(ctx - 2 * d) * tokens for d in range(1, hops + 1)]
        starts += [(partner - 2 * d) * tokens for d in range(1, hops + 1)]
        fill_bias(bias, start_ref, starts, tokens)
        products(0, s_a, d_a)

    @pl.when(reached)
    def _():
        products(2 * i + 1, s_b, d_b)
        weights(2 * i, 0, s_a, d_a)
        products(jnp.minimum(2 * i + 2, chunks - 1), s_a, d_a)
        weights(2 * i + 1, 1, s_b, d_b)

    @pl.when(reached & (i % steps == steps - 1))
    def _():
        gradients()

    @pl.when(reached & (i == pl.num_programs(0) - 1))
    def _():
        join_heads(dk, dv, part_refs, wide, tokens, heads, width**-0.5)

    @pl.when(jnp.logical_not(reached))
    def _():
        these = pl.ds(first, 2 * chunk)
        ds_ref[these, :] = jnp.zeros((2 * chunk, ds_ref.shape[1]), bf16)
        share_ref[these, :] = jnp.ones((2 * chunk, 128), f32)
        shift_ref[these, :] = jnp.zeros((2 * chunk, 128), f32)

    @pl.when(jnp.logical_not(reached) & (i == 0))
    def _():
        k_ref[...] = jnp.zeros_like(k_ref)
        for part in part_refs:
            part[...] = jnp.zeros_like(part)


def tail_kernel(
    sizes, share_ref, shift_ref, k1_ref, k2_ref, qt_ref, dot_ref, w1_ref, u1_ref, ds2_ref,
    dq_ref, own_ref, partner_ref,
    wide, w_a, ds_a, w_b, ds_b, dk, dv,
):
    tokens, groups, heads, width, per, kept = sizes
    chunk = per * tokens
    i = pl.program_id(0)
    scale = width**-0.5
    h = i * 2 * per // groups
    first = step_rows(kept, 2 * chunk)

    @pl.when(i == 0)
    def _():
        dk[...] = jnp.zeros_like(dk)
        dv[...] = jnp.zeros_like(dv)

    def rescaled(half, w_s, ds_s):
        for g in range(per):
            rows = slice(g * tokens, (g + 1) * tokens)
            here = pl.ds(first + half * chunk + g * tokens, tokens)
            w = w1_ref[here, :].astype(f32)
            share = spread(share_ref[here, :], w.shape[1])
            shift = spread(shift_ref[here, :], w.shape[1])
            w_s[rows, :] = (w * share).astype(bf16)
            ds_s[rows, :] = ((u1_ref[here, :].astype(f32) + w * shift) * share).astype(bf16)

    def gradients(half, w_s, ds_s):
        these = pl.ds(first + half * chunk, chunk)
        dk[h] += jnp.dot(qt_ref[:, these], ds_s[...], preferred_element_type=f32)
        dv[h] += jnp.dot(dot_ref[:, these], w_s[...], preferred_element_type=f32)
        dq = jnp.dot(ds_s[...], k1_ref[h], preferred_element_type=f32)
        dq += jnp.dot(ds2_ref[these, :], k2_ref[h], preferred_element_type=f32)
        dq *= scale
        group = (i * 2 + half) * per % groups
        for g in range(per):
            dq_ref[pl.ds((group + g) * heads + h, tokens, stride=groups * heads), :] = dq[
                g * tokens : (g + 1) * tokens
            ]

    rescaled(0, w_a, ds_a)
    rescaled(1, w_b, ds_b)
    gradients(0, w_a, ds_a)
    gradients(1, w_b, ds_b)

    @pl.when(i == pl.num_programs(0) - 1)
    def _():
        join_heads(dk, dv, (own_ref, partner_ref), wide, tokens, heads, scale)


def whole(*shape):
    return pl.BlockSpec(shape, lambda i: (0,) * len(shape))


def stepped(kept, *shape):
    return VMEM if kept else pl.BlockSpec(shape, lambda i: (i, 0))


def across(kept, *shape):
    return VMEM if kept else pl.BlockSpec(shape, lambda i: (0, i))


def params(kept):
    return pltpu.CompilerParams(vmem_limit_bytes=(16 if kept else 60) * 2**20)


def step_rows(kept, rows):
    if not kept:
        return 0
    return pl.multiple_of(pl.program_id(0) * rows, rows)


def prep(q, do, sizes):
    tokens, groups, heads, width, per, kept = sizes
    rows = tokens * groups * heads
    pieces = 4
    return pl.pallas_call(
        functools.partial(prep_kernel, sizes),
        in_specs=[pl.BlockSpec(memory_space=pltpu.HBM)] * 2,
        out_specs=[VMEM] * 2,
        out_shape=[jax.ShapeDtypeStruct((rows, width), bf16)] * 2,
        scratch_shapes=[
            pltpu.VMEM((2 * pieces, rows // pieces, width), f32),
            pltpu.VMEM((pieces, rows // pieces, width), bf16),
            pltpu.VMEM((pieces, rows // pieces, width), bf16),
            pltpu.SemaphoreType.DMA((pieces, 2)),
        ],
        compiler_params=params(kept),
        name="prep",
    )(q, do)


def near(qs, dos, start, own, partner, sizes):
    tokens, groups, heads, width, per, kept = sizes
    chunk = per * tokens
    rows = tokens * groups * heads
    keys = 2 * tokens
    return pl.pallas_call(
        functools.partial(near_kernel, sizes),
        grid=(rows // (2 * chunk),),
        in_specs=[VMEM] * 5,
        out_specs=[
            stepped(kept, 2 * chunk, keys),
            stepped(kept, 2 * chunk, keys),
            whole(heads, keys, width),
            stepped(kept, 2 * chunk, 128),
            stepped(kept, 2 * chunk, 128),
            across(kept, width, 2 * chunk),
            across(kept, width, 2 * chunk),
        ],
        out_shape=[
            jax.ShapeDtypeStruct((rows, keys), bf16),
            jax.ShapeDtypeStruct((rows, keys), bf16),
            jax.ShapeDtypeStruct((heads, keys, width), bf16),
            jax.ShapeDtypeStruct((rows, 128), f32),
            jax.ShapeDtypeStruct((rows, 128), f32),
            jax.ShapeDtypeStruct((width, rows), bf16),
            jax.ShapeDtypeStruct((width, rows), bf16),
        ],
        scratch_shapes=[
            pltpu.VMEM((tokens * heads, width), f32),
            pltpu.VMEM((heads, keys, width), bf16),
            pltpu.VMEM((tokens, keys), f32),
        ]
        + [pltpu.VMEM((chunk, keys), f32)] * 4,
        compiler_params=params(kept),
        cost_estimate=pl.CostEstimate(
            flops=2 * 2 * rows * (keys) * width,
            bytes_accessed=8 * rows * (keys),
            transcendentals=rows * (keys),
        ),
        name="near",
    )(qs, dos, start, own, partner)


def far(start, log1, mean1, qs, dos, qt, dt, pairs, sizes):
    tokens, groups, heads, width, per, kept = sizes
    slots = len(pairs)
    chunk = per * tokens
    rows = tokens * groups * heads
    keys = slots * tokens
    return pl.pallas_call(
        functools.partial(far_kernel, (tokens, groups, heads, slots, width, per, kept)),
        grid=(rows // (2 * chunk),),
        in_specs=[VMEM] + [stepped(kept, 2 * chunk, 128)] * 2 + [VMEM] * (4 + slots),
        out_specs=[
            whole(heads, keys, width),
            stepped(kept, 2 * chunk, keys),
            stepped(kept, 2 * chunk, 128),
            stepped(kept, 2 * chunk, 128),
        ]
        + [whole(2, tokens * heads, width)] * slots,
        out_shape=[
            jax.ShapeDtypeStruct((heads, keys, width), bf16),
            jax.ShapeDtypeStruct((rows, keys), bf16),
            jax.ShapeDtypeStruct((rows, 128), f32),
            jax.ShapeDtypeStruct((rows, 128), f32),
        ]
        + [jax.ShapeDtypeStruct((2, tokens * heads, width), bf16)] * slots,
        scratch_shapes=[
            pltpu.VMEM((tokens * heads, width), f32),
            pltpu.VMEM((heads, keys, width), bf16),
            pltpu.VMEM((tokens, keys), f32),
            pltpu.VMEM((heads, width, keys), f32),
            pltpu.VMEM((heads, width, keys), f32),
        ]
        + [pltpu.VMEM((chunk, keys), f32)] * 4
        + [pltpu.VMEM((groups * tokens, keys), bf16)] * (1 if kept else 2),
        compiler_params=params(kept),
        cost_estimate=pl.CostEstimate(
            flops=2 * 4 * rows * (keys) * width,
            bytes_accessed=8 * rows * (keys),
            transcendentals=rows * (keys),
        ),
        input_output_aliases={1: 2, 2: 3},
        name="far",
    )(start, log1, mean1, qs, dos, qt, dt, *pairs)


def tail(share, shift, k1, k2, qt, dt, w1, u1, ds2, sizes):
    tokens, groups, heads, width, per, kept = sizes
    chunk = per * tokens
    rows = tokens * groups * heads
    near_keys, far_keys = k1.shape[1], k2.shape[1]
    return pl.pallas_call(
        functools.partial(tail_kernel, sizes),
        grid=(rows // (2 * chunk),),
        in_specs=[
            stepped(kept, 2 * chunk, 128),
            stepped(kept, 2 * chunk, 128),
            whole(heads, near_keys, width),
            whole(heads, far_keys, width),
            across(kept, width, 2 * chunk),
            across(kept, width, 2 * chunk),
            stepped(kept, 2 * chunk, near_keys),
            stepped(kept, 2 * chunk, near_keys),
            stepped(kept, 2 * chunk, far_keys),
        ],
        out_specs=[VMEM] * 3,
        out_shape=[
            jax.ShapeDtypeStruct((rows, width), f32),
            jax.ShapeDtypeStruct((2, tokens * heads, width), f32),
            jax.ShapeDtypeStruct((2, tokens * heads, width), bf16),
        ],
        scratch_shapes=[
            pltpu.VMEM((tokens * heads, width), f32),
            *[pltpu.VMEM((chunk, near_keys), bf16)] * 4,
            pltpu.VMEM((heads, width, near_keys), f32),
            pltpu.VMEM((heads, width, near_keys), f32),
        ],
        compiler_params=params(kept),
        cost_estimate=pl.CostEstimate(
            flops=2 * 3 * rows * (near_keys + far_keys) * width,
            bytes_accessed=8 * rows * (near_keys + far_keys),
            transcendentals=rows * (near_keys + far_keys),
        ),
        name="tail",
    )(share, shift, k1, k2, qt, dt, w1, u1, ds2)


def shards(queries, keys, values, output_gradient, band_start):
    tokens, heads, groups, width = queries.shape
    count = lax.axis_size("ctx")
    reach = min(WINDOW // tokens, count - 1)
    hops = min((reach + 1) // 2, count // 2 - 1)
    own = jnp.stack([keys.reshape(tokens * heads, width), values.reshape(tokens * heads, width)], 0)
    same = [moved(own, 2 * d) for d in range(1, hops + 1)]
    partner = swapped(own)
    start = band_start.reshape(1, tokens)
    per = next(n for n in (3, 2, 1) if groups % (2 * n) == 0 and n * hops <= 4)
    kept = hops <= 2
    sizes = (tokens, groups, heads, width, per, kept)

    def flat(a):
        return a.transpose(0, 2, 1, 3).reshape(tokens * groups * heads, width)

    in_hbm = [
        pltpu.with_memory_space_constraint(flat(a), pltpu.HBM) for a in (queries, output_gradient)
    ]
    qs, dos = prep(*in_hbm, sizes)
    w1, u1, k1, log1, mean1, qt, dt = near(qs, dos, start, own, partner, sizes)
    *same, log1 = lax.optimization_barrier((*same, log1))
    other = [swapped(block) for block in same]
    k2, ds2, share, shift, *parts = far(
        start, log1, mean1, qs, dos, qt, dt, same + other, sizes
    )
    arriving = []
    for d in range(hops):
        crossed = swapped(parts[hops + d])
        both = (parts[d].astype(f32) + crossed.astype(f32)).astype(bf16)
        both, share = lax.optimization_barrier((both, share))
        arriving.append(moved(both, -2 * (d + 1)))
    dq, total, crossing = tail(share, shift, k1, k2, qt, dt, w1, u1, ds2, sizes)
    crossing, *arriving = lax.optimization_barrier((crossing, *arriving))
    total = total + swapped(crossing).astype(f32)
    for part in arriving:
        total = total + part.astype(f32)
    return (
        dq.reshape(tokens, groups, heads, width).transpose(0, 2, 1, 3),
        total[0].reshape(tokens, heads, width),
        total[1].reshape(tokens, heads, width),
    )


def solution(mesh):
    rows = P(("rep", "ctx"), "kv", None, None)
    keys = P(("rep", "ctx"), "kv", None)
    return jax.shard_map(
        shards,
        mesh=mesh,
        in_specs=(rows, keys, keys, rows, P(("rep", "ctx"))),
        out_specs=(rows, keys, keys),
        check_vma=False,
    )
```

```python
import functools

import jax
import jax.numpy as jnp
from jax import lax
from jax.experimental import pallas as pl
from jax.experimental.pallas import tpu as pltpu
from jax.sharding import PartitionSpec as P

WINDOW = 2048
LOG2E = 1.4426950408889634
MASKED = -1e30
f32 = jnp.float32
bf16 = jnp.bfloat16
ACROSS = (((1,), (1,)), ((), ()))
VMEM = pl.BlockSpec(memory_space=pltpu.VMEM)


def moved(block, distance):
    devices = range(lax.axis_size("ctx"))
    route = [(i - distance, i) for i in devices if i - distance in devices]
    return lax.ppermute(block, "ctx", route)


def swapped(block):
    return lax.ppermute(block, "ctx", [(i, i ^ 1) for i in range(lax.axis_size("ctx"))])


def split_heads(pair_refs, k_s, v_s, tokens, heads):
    for slot, pair in enumerate(pair_refs):
        for h in range(heads):
            rows = slice(h * tokens, (h + 1) * tokens)
            k_s[h, slot * tokens : (slot + 1) * tokens, :] = pair[0, rows, :]
            v_s[h, slot * tokens : (slot + 1) * tokens, :] = pair[1, rows, :]


def join_heads(dk, dv, part_refs, tokens, heads, scale):
    for source, grad in ((0, dk), (1, dv)):
        for slot, part in enumerate(part_refs):
            for h in range(heads):
                block = grad[h, :, slot * tokens : (slot + 1) * tokens].T
                if source == 0:
                    block *= scale
                part[source, h * tokens : (h + 1) * tokens, :] = block.astype(part.dtype)


def pack_kernel(heads, k_ref, v_ref, pair_ref, narrow, wide, arrived):
    tokens = k_ref.shape[0] // heads
    loads = [
        pltpu.make_async_copy(ref, narrow.at[source], arrived.at[source])
        for source, ref in ((0, k_ref), (1, v_ref))
    ]
    for load in loads:
        load.start()
    for source in range(2):
        loads[source].wait()
        wide[source] = narrow[source].astype(f32)
        for h in range(heads):
            pair_ref[source, h * tokens : (h + 1) * tokens, :] = wide[
                source, pl.ds(h, tokens, stride=heads), :
            ].astype(bf16)


def finish_kernel(heads, own_ref, crossed_k_ref, crossed_v_ref, *refs):
    tokens = own_ref.shape[1] // heads
    for source, crossed in ((0, crossed_k_ref), (1, crossed_v_ref)):
        for h in range(heads):
            rows = slice(h * tokens, (h + 1) * tokens)
            total = own_ref[source, rows, :] + crossed[rows, :].astype(f32)
            for arrived in refs[:-2]:
                total += arrived[source, rows, :].astype(f32)
            refs[source - 2][pl.ds(h, tokens, stride=heads), :] = total


def fill_bias(bias, start_ref, first_keys, tokens):
    down = lax.broadcasted_iota(jnp.int32, (tokens, tokens), 0)
    along = lax.broadcasted_iota(jnp.int32, (tokens, tokens), 1)
    start = jnp.sum(
        jnp.where(down == along, start_ref[...].astype(f32), 0.0), -1, keepdims=True
    ).astype(jnp.int32)
    row = lax.axis_index("ctx") * tokens + lax.broadcasted_iota(jnp.int32, (tokens, 1), 0)
    for slot, first in enumerate(first_keys):
        key = first + lax.broadcasted_iota(jnp.int32, (1, tokens), 1)
        bias[:, slot * tokens : (slot + 1) * tokens] = jnp.where(
            (key <= row) & (key >= start), 0.0, MASKED
        )


def spread(lanes, width):
    return jnp.concatenate([lanes] * (width // lanes.shape[1]), 1)


def prep_kernel(sizes, q_ref, do_ref, qs_ref, dos_ref, wide, q_in, do_in, arrived):
    tokens, groups, heads, width, here, kept = sizes
    pieces = q_in.shape[0]
    size = tokens // pieces * groups * heads
    blocks = tokens // here
    loads = []
    for n in range(pieces):
        for k, (source, target) in enumerate(((q_ref, q_in), (do_ref, do_in))):
            load = pltpu.make_async_copy(
                source.at[pl.ds(n * size, size), :], target.at[n], arrived.at[n, k]
            )
            load.start()
            loads.append(load)
    for n in range(pieces):
        for k, (source, split) in enumerate(((q_in, qs_ref), (do_in, dos_ref))):
            loads[2 * n + k].wait()
            wide[2 * n + k] = source[n].astype(f32)
            for h in range(heads):
                for b in range(blocks // pieces):
                    for g in range(groups):
                        at = ((h * blocks + n * (blocks // pieces) + b) * groups + g) * here
                        begin = (b * here * groups + g) * heads + h
                        split[at : at + here, :] = wide[
                            2 * n + k, pl.ds(begin, here, stride=groups * heads), :
                        ].astype(bf16)


def near_kernel(
    sizes, qs, dos, start_ref, own_ref, partner_ref,
    w_ref, u_ref, k_ref, log_ref, mean_ref, qt_ref, dot_ref,
    v_s, bias, s_a, d_a, s_b, d_b,
):
    tokens, groups, heads, width, here, kept = sizes
    chunk = here * groups
    blocks = tokens // here
    chunks = blocks * heads
    i = pl.program_id(0)
    first = step_rows(kept, 2 * chunk)
    slope = width**-0.5 * LOG2E
    lower, every = tokens + tokens // 2, 2 * tokens
    early = i % (blocks // 2) < blocks // 4

    def products(c, s, d, keys):
        rows = pl.ds(pl.multiple_of(c * chunk, chunk), chunk)
        h = c // blocks
        s[:, :keys] = lax.dot_general(qs[rows, :], k_ref[h, :keys], ACROSS, preferred_element_type=f32)
        d[:, :keys] = lax.dot_general(dos[rows, :], v_s[h, :keys], ACROSS, preferred_element_type=f32)

    def weights(c, half, s, d, keys):
        size = chunk // 3
        band = bias[pl.ds(pl.multiple_of(c % blocks * here, here), here), :keys]
        band = jnp.concatenate([band] * (size // here), 0)
        for row in range(0, chunk, size):
            rows = slice(row, row + size)
            out = pl.ds(first + half * chunk + row, size)
            x = s[rows, :keys] * slope + band
            dp = d[rows, :keys]
            m = jnp.max(x, -1, keepdims=True)
            p = jnp.exp2(x - m)
            total = jnp.sum(p, -1, keepdims=True)
            inverse = 1.0 / total
            dot = jnp.sum(p * dp, -1, keepdims=True) * inverse
            w = p * inverse
            w_ref[out, :keys] = w.astype(bf16)
            u_ref[out, :keys] = (w * (dp - dot)).astype(bf16)
            log_ref[out, :] = jnp.broadcast_to(m + jnp.log2(total), (size, 128))
            mean_ref[out, :] = jnp.broadcast_to(dot, (size, 128))

    @pl.when(i == 0)
    def _():
        split_heads((partner_ref, own_ref), k_ref, v_s, tokens, heads)
        ctx = lax.axis_index("ctx")
        fill_bias(bias, start_ref, ((ctx + 1 - 2 * (ctx % 2)) * tokens, ctx * tokens), tokens)
        products(0, s_a, d_a, lower)

    both = pl.ds(pl.multiple_of(i * 2 * chunk, 2 * chunk), 2 * chunk)
    columns = pl.ds(first, 2 * chunk)

    def step(keys, next_keys):
        products(2 * i + 1, s_b, d_b, keys)
        qt_ref[:, columns] = qs[both, :].T
        weights(2 * i, 0, s_a, d_a, keys)
        products(jnp.minimum(2 * i + 2, chunks - 1), s_a, d_a, next_keys)
        dot_ref[:, columns] = dos[both, :].T
        weights(2 * i + 1, 1, s_b, d_b, keys)

    @pl.when(early)
    def _():
        step(lower, every)

    @pl.when(jnp.logical_not(early))
    def _():
        step(every, lower if blocks == 4 else every)


def far_kernel(
    sizes, start_ref, log1_ref, mean1_ref, qs_ref, dos_ref, qt_ref, dot_ref, *refs,
):
    tokens, groups, heads, slots, width, here, kept = sizes
    pair_refs = refs[:slots]
    k_ref, ds_ref, share_ref, shift_ref = refs[slots : slots + 4]
    part_refs = refs[slots + 4 : 2 * slots + 4]
    v_s, bias, dk, dv, s_a, d_a, s_b, d_b, w_s = refs[2 * slots + 4 :]
    chunk = here * groups
    blocks = tokens // here
    chunks = blocks * heads
    hops = slots // 2
    i = pl.program_id(0)
    first = step_rows(kept, 2 * chunk)
    slope = width**-0.5 * LOG2E
    ctx = lax.axis_index("ctx")
    reached = ctx >= 2
    steps = blocks // 2
    inside = pl.multiple_of(i % steps * 2 * chunk, 2 * chunk) if kept else 0

    def products(c, s, d):
        rows = pl.ds(pl.multiple_of(c * chunk, chunk), chunk)
        h = c // blocks
        s[...] = lax.dot_general(qs_ref[rows, :], k_ref[h], ACROSS, preferred_element_type=f32)
        d[...] = lax.dot_general(dos_ref[rows, :], v_s[h], ACROSS, preferred_element_type=f32)

    def gradients(count):
        h = i // steps
        rows = pl.ds(pl.multiple_of((i - count + 1) * 2 * chunk, 2 * chunk), count * 2 * chunk)
        ds = ds_ref[rows, :] if kept else ds_ref[...]
        dk_part = jnp.dot(qt_ref[:, rows], ds, preferred_element_type=f32)
        dv_part = jnp.dot(dot_ref[:, rows], w_s[...], preferred_element_type=f32)
        if kept:
            dk[h] = dk_part
            dv[h] = dv_part
        else:
            dk[h] += dk_part
            dv[h] += dv_part

    def weights(c, half, s, d):
        size = chunk // 3
        band = bias[pl.ds(pl.multiple_of(c % blocks * here, here), here), :]
        band = jnp.concatenate([band] * (size // here), 0)
        for row in range(0, chunk, size):
            rows = slice(row, row + size)
            out = pl.ds(first + half * chunk + row, size)
            log1 = log1_ref[out, :]
            mean1 = mean1_ref[out, :]
            x = s[rows, :] * slope + band
            dp = d[rows, :]
            m = jnp.maximum(jnp.max(x, -1, keepdims=True), log1)
            p = jnp.exp2(x - spread(m, x.shape[1]))
            before = jnp.exp2(log1 - m)
            inverse = 1.0 / (jnp.sum(p, -1, keepdims=True) + before)
            mean = (jnp.sum(p * dp, -1, keepdims=True) + before * mean1) * inverse
            w = p * spread(inverse, x.shape[1])
            ds = (w * (dp - spread(mean, x.shape[1]))).astype(bf16)
            there = pl.ds(inside + half * chunk + row, size)
            w_s[there, :] = w.astype(bf16)
            ds_ref[out, :] = ds
            share_ref[out, :] = before * inverse
            shift_ref[out, :] = mean1 - mean

    @pl.when(reached & (i == 0))
    def _():
        split_heads(pair_refs, k_ref, v_s, tokens, heads)
        partner = ctx + 1 - 2 * (ctx % 2)
        starts = [(ctx - 2 * d) * tokens for d in range(1, hops + 1)]
        starts += [(partner - 2 * d) * tokens for d in range(1, hops + 1)]
        fill_bias(bias, start_ref, starts, tokens)
        if not kept:
            dk[...] = jnp.zeros_like(dk)
            dv[...] = jnp.zeros_like(dv)
        products(0, s_a, d_a)

    @pl.when(reached)
    def _():
        products(2 * i + 1, s_b, d_b)
        weights(2 * i, 0, s_a, d_a)
        products(jnp.minimum(2 * i + 2, chunks - 1), s_a, d_a)
        weights(2 * i + 1, 1, s_b, d_b)

    if kept:
        pl.when(reached & (i % steps == steps - 1))(lambda: gradients(steps))
    else:
        pl.when(reached)(lambda: gradients(1))

    @pl.when(reached & (i == pl.num_programs(0) - 1))
    def _():
        join_heads(dk, dv, part_refs, tokens, heads, width**-0.5)

    @pl.when(jnp.logical_not(reached))
    def _():
        these = pl.ds(first, 2 * chunk)
        ds_ref[these, :] = jnp.zeros((2 * chunk, ds_ref.shape[1]), bf16)
        share_ref[these, :] = jnp.ones((2 * chunk, 128), f32)
        shift_ref[these, :] = jnp.zeros((2 * chunk, 128), f32)

    @pl.when(jnp.logical_not(reached) & (i == 0))
    def _():
        k_ref[...] = jnp.zeros_like(k_ref)
        for part in part_refs:
            part[...] = jnp.zeros_like(part)


def tail_kernel(
    sizes, k1_ref, k2_ref, share_ref, shift_ref, w1_ref, u1_ref, ds2_ref, *refs,
):
    tokens, groups, heads, width, here, kept = sizes
    qt_refs, dot_refs = refs[:heads], refs[heads : 2 * heads]
    dq_ref, own_ref, partner_ref, dk, dv = refs[2 * heads : 2 * heads + 5]
    scratch = refs[2 * heads + 5 :]
    chunk = here * groups
    i = pl.program_id(0)
    scale = width**-0.5
    first = step_rows(kept, chunk)

    @pl.when(i == 0)
    def _():
        dk[...] = jnp.zeros_like(dk)
        dv[...] = jnp.zeros_like(dv)

    def rescaled(h, w_s, ds_s, keys):
        size = 64 if chunk % 64 == 0 else chunk
        for row in range(0, chunk, size):
            rows = pl.ds(first + row, size)
            w = w1_ref[h, rows, :keys].astype(f32)
            share = spread(share_ref[h, rows, :], w.shape[1])
            shift = spread(shift_ref[h, rows, :], w.shape[1])
            w_s[row : row + size, :keys] = (w * share).astype(bf16)
            ds_s[row : row + size, :keys] = (
                (u1_ref[h, rows, :keys].astype(f32) + w * shift) * share
            ).astype(bf16)

    def gradients(h, w_s, ds_s, keys):
        columns = pl.ds((h * tokens * groups if kept else 0) + first, chunk)
        ds = ds_s[:, :keys]
        dk[h, :, :keys] += jnp.dot(qt_refs[h][:, columns], ds, preferred_element_type=f32)
        dv[h, :, :keys] += jnp.dot(
            dot_refs[h][:, columns], w_s[:, :keys], preferred_element_type=f32
        )
        dq = jnp.dot(ds, k1_ref[h, :keys], preferred_element_type=f32)
        dq += jnp.dot(ds2_ref[h, pl.ds(first, chunk), :], k2_ref[h], preferred_element_type=f32)
        dq *= scale
        for g in range(groups):
            dq_ref[pl.ds(g * heads + h, here, stride=groups * heads), :] = dq[
                g * here : (g + 1) * here
            ]

    def step(keys):
        for h in range(heads):
            rescaled(h, scratch[2 * h], scratch[2 * h + 1], keys)
        for h in range(heads):
            gradients(h, scratch[2 * h], scratch[2 * h + 1], keys)

    half = pl.num_programs(0) // 2
    pl.when(i < half)(lambda: step(tokens + tokens // 2))
    pl.when(i >= half)(lambda: step(2 * tokens))

    @pl.when(i == pl.num_programs(0) - 1)
    def _():
        join_heads(dk, dv, (partner_ref, own_ref), tokens, heads, scale)


def pack(keys, values, heads):
    return pl.pallas_call(
        functools.partial(pack_kernel, heads),
        in_specs=[pl.BlockSpec(memory_space=pltpu.HBM)] * 2,
        out_specs=VMEM,
        out_shape=jax.ShapeDtypeStruct((2, *keys.shape), bf16),
        scratch_shapes=[
            pltpu.VMEM((2, *keys.shape), bf16),
            pltpu.VMEM((2, *keys.shape), f32),
            pltpu.SemaphoreType.DMA((2,)),
        ],
        compiler_params=params(True, 4),
        name="pack",
    )(keys, values)


def finish(own, crossed, arrived, heads):
    return pl.pallas_call(
        functools.partial(finish_kernel, heads),
        in_specs=[VMEM] * (3 + len(arrived)),
        out_specs=[VMEM] * 2,
        out_shape=[jax.ShapeDtypeStruct(own.shape[1:], f32)] * 2,
        compiler_params=params(True, 8),
        name="finish",
    )(own, *crossed, *arrived)


def whole(*shape):
    return pl.BlockSpec(shape, lambda i: (0,) * len(shape))


def stepped(kept, *shape):
    return VMEM if kept else pl.BlockSpec(shape, lambda i: (i, 0))


def across(kept, *shape):
    return VMEM if kept else pl.BlockSpec(shape, lambda i: (0, i))


def params(kept, megabytes=16):
    return pltpu.CompilerParams(vmem_limit_bytes=(megabytes if kept else 60) * 2**20)


def step_rows(kept, rows):
    if not kept:
        return 0
    return pl.multiple_of(pl.program_id(0) * rows, rows)


def prep(q, do, sizes):
    tokens, groups, heads, width, here, kept = sizes
    rows = tokens * groups * heads
    pieces = 4
    return pl.pallas_call(
        functools.partial(prep_kernel, sizes),
        in_specs=[pl.BlockSpec(memory_space=pltpu.HBM)] * 2,
        out_specs=[VMEM] * 2,
        out_shape=[jax.ShapeDtypeStruct((rows, width), bf16)] * 2,
        scratch_shapes=[
            pltpu.VMEM((2 * pieces, rows // pieces, width), f32),
            pltpu.VMEM((pieces, rows // pieces, width), bf16),
            pltpu.VMEM((pieces, rows // pieces, width), bf16),
            pltpu.SemaphoreType.DMA((pieces, 2)),
        ],
        compiler_params=params(kept),
        name="prep",
    )(q, do)


def near(qs, dos, start, own, partner, sizes):
    tokens, groups, heads, width, here, kept = sizes
    chunk = here * groups
    rows = tokens * groups * heads
    keys = 2 * tokens
    return pl.pallas_call(
        functools.partial(near_kernel, sizes),
        grid=(rows // (2 * chunk),),
        in_specs=[VMEM] * 5,
        out_specs=[
            stepped(kept, 2 * chunk, keys),
            stepped(kept, 2 * chunk, keys),
            whole(heads, keys, width),
            stepped(kept, 2 * chunk, 128),
            stepped(kept, 2 * chunk, 128),
            across(kept, width, 2 * chunk),
            across(kept, width, 2 * chunk),
        ],
        out_shape=[
            jax.ShapeDtypeStruct((rows, keys), bf16),
            jax.ShapeDtypeStruct((rows, keys), bf16),
            jax.ShapeDtypeStruct((heads, keys, width), bf16),
            jax.ShapeDtypeStruct((rows, 128), f32),
            jax.ShapeDtypeStruct((rows, 128), f32),
            jax.ShapeDtypeStruct((width, rows), bf16),
            jax.ShapeDtypeStruct((width, rows), bf16),
        ],
        scratch_shapes=[
            pltpu.VMEM((heads, keys, width), bf16),
            pltpu.VMEM((tokens, keys), f32),
        ]
        + [pltpu.VMEM((chunk, keys), f32)] * 4,
        compiler_params=params(kept),
        cost_estimate=pl.CostEstimate(
            flops=2 * 2 * rows * (keys) * width,
            bytes_accessed=8 * rows * (keys),
            transcendentals=rows * (keys),
        ),
        name="near",
    )(qs, dos, start, own, partner)


def far(start, log1, mean1, qs, dos, qt, dt, pairs, sizes):
    tokens, groups, heads, width, here, kept = sizes
    slots = len(pairs)
    chunk = here * groups
    rows = tokens * groups * heads
    keys = slots * tokens
    return pl.pallas_call(
        functools.partial(far_kernel, (tokens, groups, heads, slots, width, here, kept)),
        grid=(rows // (2 * chunk),),
        in_specs=[VMEM] + [stepped(kept, 2 * chunk, 128)] * 2 + [VMEM] * (4 + slots),
        out_specs=[
            whole(heads, keys, width),
            stepped(kept, 2 * chunk, keys),
            stepped(kept, 2 * chunk, 128),
            stepped(kept, 2 * chunk, 128),
        ]
        + [whole(2, tokens * heads, width)] * slots,
        out_shape=[
            jax.ShapeDtypeStruct((heads, keys, width), bf16),
            jax.ShapeDtypeStruct((rows, keys), bf16),
            jax.ShapeDtypeStruct((rows, 128), f32),
            jax.ShapeDtypeStruct((rows, 128), f32),
        ]
        + [jax.ShapeDtypeStruct((2, tokens * heads, width), bf16)] * slots,
        scratch_shapes=[
            pltpu.VMEM((heads, keys, width), bf16),
            pltpu.VMEM((tokens, keys), f32),
            pltpu.VMEM((heads, width, keys), f32),
            pltpu.VMEM((heads, width, keys), f32),
        ]
        + [pltpu.VMEM((chunk, keys), f32)] * 4
        + [pltpu.VMEM((groups * tokens if kept else 2 * chunk, keys), bf16)],
        compiler_params=params(kept),
        cost_estimate=pl.CostEstimate(
            flops=2 * 4 * rows * (keys) * width,
            bytes_accessed=8 * rows * (keys),
            transcendentals=rows * (keys),
        ),
        input_output_aliases={1: 2, 2: 3},
        name="far",
    )(start, log1, mean1, qs, dos, qt, dt, *pairs)


def tail(share, shift, k1, k2, qt, dt, w1, u1, ds2, sizes):
    tokens, groups, heads, width, here, kept = sizes
    chunk = here * groups
    rows = tokens * groups * heads
    blocks = tokens // here
    near_keys, far_keys = k1.shape[1], k2.shape[1]

    def both(columns):
        if kept:
            return VMEM
        return pl.BlockSpec((heads, chunk, columns), lambda i: (0, i, 0))

    def turned(h):
        if kept:
            return VMEM
        return pl.BlockSpec((width, chunk), lambda i: (0, h * blocks + i))

    def by_head(a):
        return a.reshape(heads, rows // heads, a.shape[1])

    return pl.pallas_call(
        functools.partial(tail_kernel, sizes),
        grid=(blocks,),
        in_specs=[
            whole(heads, near_keys, width),
            whole(heads, far_keys, width),
            both(128),
            both(128),
            both(near_keys),
            both(near_keys),
            both(far_keys),
        ]
        + [turned(h) for h in range(heads)] * 2,
        out_specs=[pl.BlockSpec((chunk * heads, width), lambda i: (i, 0)), VMEM, VMEM],
        out_shape=[
            jax.ShapeDtypeStruct((rows, width), f32),
            jax.ShapeDtypeStruct((2, tokens * heads, width), f32),
            jax.ShapeDtypeStruct((2, tokens * heads, width), bf16),
        ],
        scratch_shapes=[
            pltpu.VMEM((heads, width, near_keys), f32),
            pltpu.VMEM((heads, width, near_keys), f32),
            *[pltpu.VMEM((chunk, near_keys), bf16)] * (2 * heads),
        ],
        compiler_params=params(kept, 14),
        cost_estimate=pl.CostEstimate(
            flops=6 * rows * (near_keys + far_keys) * width,
            bytes_accessed=8 * rows * (near_keys + far_keys),
            transcendentals=rows * (near_keys + far_keys),
        ),
        name="tail",
    )(
        k1,
        k2,
        *[by_head(a) for a in (share, shift, w1, u1, ds2)],
        *[qt] * heads,
        *[dt] * heads,
    )


def shards(queries, keys, values, output_gradient, band_start):
    tokens, heads, groups, width = queries.shape
    count = lax.axis_size("ctx")
    reach = min(WINDOW // tokens, count - 1)
    hops = min((reach + 1) // 2, count // 2 - 1)

    def in_hbm(a):
        return pltpu.with_memory_space_constraint(a, pltpu.HBM)

    own = pack(
        in_hbm(keys.reshape(tokens * heads, width)),
        in_hbm(values.reshape(tokens * heads, width)),
        heads,
    )
    same = [moved(own, 2 * d) for d in range(1, hops + 1)]
    partner = swapped(own)
    start = band_start.reshape(1, tokens)
    kept = hops <= 2
    here = tokens // (4 if kept else 8)
    sizes = (tokens, groups, heads, width, here, kept)

    def flat(a):
        return a.transpose(0, 2, 1, 3).reshape(tokens * groups * heads, width)

    qs, dos = prep(in_hbm(flat(queries)), in_hbm(flat(output_gradient)), sizes)
    w1, u1, k1, log1, mean1, qt, dt = near(qs, dos, start, own, partner, sizes)
    *same, log1 = lax.optimization_barrier((*same, log1))
    other = [swapped(block) for block in same]
    k2, ds2, share, shift, *parts = far(
        start, log1, mean1, qs, dos, qt, dt, same + other, sizes
    )
    arriving = []
    for d in range(hops):
        crossed = swapped(parts[hops + d])
        both = (parts[d].astype(f32) + crossed.astype(f32)).astype(bf16)
        both, share = lax.optimization_barrier((both, share))
        arriving.append(moved(both, -2 * (d + 1)))
    dq, total, crossing = tail(share, shift, k1, k2, qt, dt, w1, u1, ds2, sizes)
    crossed = [swapped(half) for half in crossing]
    dk, dv = finish(total, crossed, arriving, heads)
    return (
        dq.reshape(tokens, groups, heads, width).transpose(0, 2, 1, 3),
        dk.reshape(tokens, heads, width),
        dv.reshape(tokens, heads, width),
    )


def solution(mesh):
    rows = P(("rep", "ctx"), "kv", None, None)
    keys = P(("rep", "ctx"), "kv", None)
    return jax.shard_map(
        shards,
        mesh=mesh,
        in_specs=(rows, keys, keys, rows, P(("rep", "ctx"))),
        out_specs=(rows, keys, keys),
        check_vma=False,
    )
```

```python
import functools

import jax
import jax.numpy as jnp
from jax import lax
from jax.experimental import pallas as pl
from jax.experimental.pallas import tpu as pltpu
from jax.sharding import PartitionSpec as P

WINDOW = 2048
LOG2E = 1.4426950408889634
MASKED = -1e30
f32 = jnp.float32
bf16 = jnp.bfloat16
ACROSS = (((1,), (1,)), ((), ()))
VMEM = pl.BlockSpec(memory_space=pltpu.VMEM)


def moved(block, distance):
    devices = range(lax.axis_size("ctx"))
    route = [(i - distance, i) for i in devices if i - distance in devices]
    return lax.ppermute(block, "ctx", route)


def swapped(block):
    return lax.ppermute(block, "ctx", [(i, i ^ 1) for i in range(lax.axis_size("ctx"))])


def split_heads(pair_refs, k_s, v_s, tokens, heads):
    for slot, pair in enumerate(pair_refs):
        for h in range(heads):
            rows = slice(h * tokens, (h + 1) * tokens)
            k_s[h, slot * tokens : (slot + 1) * tokens, :] = pair[0, rows, :]
            v_s[h, slot * tokens : (slot + 1) * tokens, :] = pair[1, rows, :]


def join_heads(dk, dv, part_refs, tokens, heads, scale):
    for source, grad in ((0, dk), (1, dv)):
        for slot, part in enumerate(part_refs):
            for h in range(heads):
                block = grad[h, :, slot * tokens : (slot + 1) * tokens].T
                if source == 0:
                    block *= scale
                part[source, h * tokens : (h + 1) * tokens, :] = block.astype(part.dtype)


def pack_kernel(heads, k_ref, v_ref, pair_ref, narrow, wide, arrived):
    tokens = k_ref.shape[0] // heads
    loads = [
        pltpu.make_async_copy(ref, narrow.at[source], arrived.at[source])
        for source, ref in ((0, k_ref), (1, v_ref))
    ]
    for load in loads:
        load.start()
    for source in range(2):
        loads[source].wait()
        wide[source] = narrow[source].astype(f32)
        for h in range(heads):
            pair_ref[source, h * tokens : (h + 1) * tokens, :] = wide[
                source, pl.ds(h, tokens, stride=heads), :
            ].astype(bf16)


def finish_kernel(heads, own_ref, crossed_k_ref, crossed_v_ref, *refs):
    tokens = own_ref.shape[1] // heads
    for source, crossed in ((0, crossed_k_ref), (1, crossed_v_ref)):
        for h in range(heads):
            rows = slice(h * tokens, (h + 1) * tokens)
            total = own_ref[source, rows, :] + crossed[rows, :].astype(f32)
            for arrived in refs[:-2]:
                total += arrived[source, rows, :].astype(f32)
            refs[source - 2][pl.ds(h, tokens, stride=heads), :] = total


def fill_bias(bias, start_ref, first_keys, tokens):
    down = lax.broadcasted_iota(jnp.int32, (tokens, tokens), 0)
    along = lax.broadcasted_iota(jnp.int32, (tokens, tokens), 1)
    start = jnp.sum(
        jnp.where(down == along, start_ref[...].astype(f32), 0.0), -1, keepdims=True
    ).astype(jnp.int32)
    row = lax.axis_index("ctx") * tokens + lax.broadcasted_iota(jnp.int32, (tokens, 1), 0)
    for slot, first in enumerate(first_keys):
        key = first + lax.broadcasted_iota(jnp.int32, (1, tokens), 1)
        bias[:, slot * tokens : (slot + 1) * tokens] = jnp.where(
            (key <= row) & (key >= start), 0.0, MASKED
        )


def spread(lanes, width):
    return jnp.concatenate([lanes] * (width // lanes.shape[1]), 1)


def prep_kernel(sizes, q_ref, do_ref, qs_ref, dos_ref, wide, q_in, do_in, arrived):
    tokens, groups, heads, width, here, kept = sizes
    pieces = q_in.shape[0]
    size = tokens // pieces * groups * heads
    blocks = tokens // here
    loads = []
    for n in range(pieces):
        for k, (source, target) in enumerate(((q_ref, q_in), (do_ref, do_in))):
            load = pltpu.make_async_copy(
                source.at[pl.ds(n * size, size), :], target.at[n], arrived.at[n, k]
            )
            load.start()
            loads.append(load)
    for n in range(pieces):
        for k, (source, split) in enumerate(((q_in, qs_ref), (do_in, dos_ref))):
            loads[2 * n + k].wait()
            wide[2 * n + k] = source[n].astype(f32)
            for h in range(heads):
                for b in range(blocks // pieces):
                    for g in range(groups):
                        at = ((h * blocks + n * (blocks // pieces) + b) * groups + g) * here
                        begin = (b * here * groups + g) * heads + h
                        split[at : at + here, :] = wide[
                            2 * n + k, pl.ds(begin, here, stride=groups * heads), :
                        ].astype(bf16)


def near_kernel(
    sizes, qs, dos, start_ref, own_ref, partner_ref,
    w_ref, u_ref, k_ref, log_ref, mean_ref, qt_ref, dot_ref,
    v_s, bias, s_a, d_a, s_b, d_b,
):
    tokens, groups, heads, width, here, kept = sizes
    chunk = here * groups
    blocks = tokens // here
    chunks = blocks * heads
    i = pl.program_id(0)
    first = step_rows(kept, 2 * chunk)
    slope = width**-0.5 * LOG2E
    lower, every = tokens + tokens // 2, 2 * tokens
    early = i % (blocks // 2) < blocks // 4

    def products(c, s, d, keys):
        rows = pl.ds(pl.multiple_of(c * chunk, chunk), chunk)
        h = c // blocks
        s[:, :keys] = lax.dot_general(qs[rows, :], k_ref[h, :keys], ACROSS, preferred_element_type=f32)
        d[:, :keys] = lax.dot_general(dos[rows, :], v_s[h, :keys], ACROSS, preferred_element_type=f32)

    def weights(c, half, s, d, keys):
        size = chunk // 3
        band = bias[pl.ds(pl.multiple_of(c % blocks * here, here), here), :keys]
        band = jnp.concatenate([band] * (size // here), 0)
        for row in range(0, chunk, size):
            rows = slice(row, row + size)
            out = pl.ds(first + half * chunk + row, size)
            x = s[rows, :keys] * slope + band
            dp = d[rows, :keys]
            m = jnp.max(x, -1, keepdims=True)
            p = jnp.exp2(x - m)
            total = jnp.sum(p, -1, keepdims=True)
            inverse = 1.0 / total
            dot = jnp.sum(p * dp, -1, keepdims=True) * inverse
            w = p * inverse
            w_ref[out, :keys] = w.astype(bf16)
            u_ref[out, :keys] = (w * (dp - dot)).astype(bf16)
            log_ref[out, :] = jnp.broadcast_to(m + jnp.log2(total), (size, 128))
            mean_ref[out, :] = jnp.broadcast_to(dot, (size, 128))

    @pl.when(i == 0)
    def _():
        split_heads((partner_ref, own_ref), k_ref, v_s, tokens, heads)
        ctx = lax.axis_index("ctx")
        fill_bias(bias, start_ref, ((ctx + 1 - 2 * (ctx % 2)) * tokens, ctx * tokens), tokens)
        products(0, s_a, d_a, lower)

    both = pl.ds(pl.multiple_of(i * 2 * chunk, 2 * chunk), 2 * chunk)
    columns = pl.ds(first, 2 * chunk)

    def step(keys, next_keys):
        products(2 * i + 1, s_b, d_b, keys)
        qt_ref[:, columns] = qs[both, :].T
        weights(2 * i, 0, s_a, d_a, keys)
        products(jnp.minimum(2 * i + 2, chunks - 1), s_a, d_a, next_keys)
        dot_ref[:, columns] = dos[both, :].T
        weights(2 * i + 1, 1, s_b, d_b, keys)

    @pl.when(early)
    def _():
        step(lower, every)

    @pl.when(jnp.logical_not(early))
    def _():
        step(every, lower if blocks == 4 else every)


def far_kernel(
    sizes, start_ref, log1_ref, mean1_ref, qs_ref, dos_ref, qt_ref, dot_ref, *refs,
):
    tokens, groups, heads, slots, width, here, kept = sizes
    pair_refs = refs[:slots]
    k_ref, ds_ref, share_ref, shift_ref = refs[slots : slots + 4]
    part_refs = refs[slots + 4 : 2 * slots + 4]
    v_s, bias, dk, dv, s_a, d_a, s_b, d_b, w_s = refs[2 * slots + 4 :]
    chunk = here * groups
    blocks = tokens // here
    chunks = blocks * heads
    hops = slots // 2
    i = pl.program_id(0)
    first = step_rows(kept, 2 * chunk)
    slope = width**-0.5 * LOG2E
    ctx = lax.axis_index("ctx")
    reached = ctx >= 2
    steps = blocks // 2
    inside = pl.multiple_of(i % steps * 2 * chunk, 2 * chunk) if kept else 0

    def products(c, s, d):
        rows = pl.ds(pl.multiple_of(c * chunk, chunk), chunk)
        h = c // blocks
        s[...] = lax.dot_general(qs_ref[rows, :], k_ref[h], ACROSS, preferred_element_type=f32)
        d[...] = lax.dot_general(dos_ref[rows, :], v_s[h], ACROSS, preferred_element_type=f32)

    def gradients(count):
        h = i // steps
        rows = pl.ds(pl.multiple_of((i - count + 1) * 2 * chunk, 2 * chunk), count * 2 * chunk)
        ds = ds_ref[rows, :] if kept else ds_ref[...]
        dk_part = jnp.dot(qt_ref[:, rows], ds, preferred_element_type=f32)
        dv_part = jnp.dot(dot_ref[:, rows], w_s[...], preferred_element_type=f32)
        if kept:
            dk[h] = dk_part
            dv[h] = dv_part
        else:
            dk[h] += dk_part
            dv[h] += dv_part

    def weights(c, half, s, d):
        size = chunk // 3
        band = bias[pl.ds(pl.multiple_of(c % blocks * here, here), here), :]
        band = jnp.concatenate([band] * (size // here), 0)
        for row in range(0, chunk, size):
            rows = slice(row, row + size)
            out = pl.ds(first + half * chunk + row, size)
            log1 = log1_ref[out, :]
            mean1 = mean1_ref[out, :]
            x = s[rows, :] * slope + band
            dp = d[rows, :]
            m = jnp.maximum(jnp.max(x, -1, keepdims=True), log1)
            p = jnp.exp2(x - spread(m, x.shape[1]))
            before = jnp.exp2(log1 - m)
            inverse = 1.0 / (jnp.sum(p, -1, keepdims=True) + before)
            mean = (jnp.sum(p * dp, -1, keepdims=True) + before * mean1) * inverse
            w = p * spread(inverse, x.shape[1])
            ds = (w * (dp - spread(mean, x.shape[1]))).astype(bf16)
            there = pl.ds(inside + half * chunk + row, size)
            w_s[there, :] = w.astype(bf16)
            ds_ref[out, :] = ds
            share_ref[out, :] = before * inverse
            shift_ref[out, :] = mean1 - mean

    @pl.when(reached & (i == 0))
    def _():
        split_heads(pair_refs, k_ref, v_s, tokens, heads)
        partner = ctx + 1 - 2 * (ctx % 2)
        starts = [(ctx - 2 * d) * tokens for d in range(1, hops + 1)]
        starts += [(partner - 2 * d) * tokens for d in range(1, hops + 1)]
        fill_bias(bias, start_ref, starts, tokens)
        if not kept:
            dk[...] = jnp.zeros_like(dk)
            dv[...] = jnp.zeros_like(dv)
        products(0, s_a, d_a)

    @pl.when(reached)
    def _():
        products(2 * i + 1, s_b, d_b)
        weights(2 * i, 0, s_a, d_a)
        products(jnp.minimum(2 * i + 2, chunks - 1), s_a, d_a)
        weights(2 * i + 1, 1, s_b, d_b)

    if kept:
        pl.when(reached & (i % steps == steps - 1))(lambda: gradients(steps))
    else:
        pl.when(reached)(lambda: gradients(1))

    @pl.when(reached & (i == pl.num_programs(0) - 1))
    def _():
        join_heads(dk, dv, part_refs, tokens, heads, width**-0.5)

    @pl.when(jnp.logical_not(reached))
    def _():
        these = pl.ds(first, 2 * chunk)
        ds_ref[these, :] = jnp.zeros((2 * chunk, ds_ref.shape[1]), bf16)
        share_ref[these, :] = jnp.ones((2 * chunk, 128), f32)
        shift_ref[these, :] = jnp.zeros((2 * chunk, 128), f32)

    @pl.when(jnp.logical_not(reached) & (i == 0))
    def _():
        k_ref[...] = jnp.zeros_like(k_ref)
        for part in part_refs:
            part[...] = jnp.zeros_like(part)


def ahead_kernel(k_ref, ds_ref, dq_ref):
    heads = k_ref.shape[0]
    each = ds_ref.shape[0] // heads
    for h in range(heads):
        rows = slice(h * each, h * each + (each if h < heads - 1 else each // 2))
        dq_ref[rows, :] = jnp.dot(ds_ref[rows, :], k_ref[h], preferred_element_type=f32)


def tail_kernel(
    sizes, k1_ref, k2_ref, share_ref, shift_ref, w1_ref, u1_ref, ds2_ref, *refs,
):
    tokens, groups, heads, width, here, kept = sizes
    qt_refs, dot_refs = refs[:heads], refs[heads : 2 * heads]
    ahead_ref = refs[2 * heads]
    dq_ref, own_ref, partner_ref, dk, dv, *scratch = refs[2 * heads + (1 if kept else 0) :]
    chunk = here * groups
    i = pl.program_id(0)
    scale = width**-0.5
    first = step_rows(kept, chunk)

    @pl.when(i == 0)
    def _():
        dk[...] = jnp.zeros_like(dk)
        dv[...] = jnp.zeros_like(dv)

    def rescaled(h, w_s, ds_s, keys):
        size = 64 if chunk % 64 == 0 else chunk
        for row in range(0, chunk, size):
            rows = pl.ds(first + row, size)
            w = w1_ref[h, rows, :keys].astype(f32)
            share = spread(share_ref[h, rows, :], w.shape[1])
            shift = spread(shift_ref[h, rows, :], w.shape[1])
            w_s[row : row + size, :keys] = (w * share).astype(bf16)
            ds_s[row : row + size, :keys] = (
                (u1_ref[h, rows, :keys].astype(f32) + w * shift) * share
            ).astype(bf16)

    def gradients(h, w_s, ds_s, keys):
        columns = pl.ds((h * tokens * groups if kept else 0) + first, chunk)
        ds = ds_s[:, :keys]
        dk[h, :, :keys] += jnp.dot(qt_refs[h][:, columns], ds, preferred_element_type=f32)
        dv[h, :, :keys] += jnp.dot(
            dot_refs[h][:, columns], w_s[:, :keys], preferred_element_type=f32
        )
        dq = jnp.dot(ds, k1_ref[h, :keys], preferred_element_type=f32)
        if kept and (h < heads - 1 or keys < 2 * tokens):
            dq += ahead_ref[pl.ds(h * groups * tokens + first, chunk), :]
        else:
            dq += jnp.dot(
                ds2_ref[h, pl.ds(first, chunk), :], k2_ref[h], preferred_element_type=f32
            )
        dq *= scale
        for g in range(groups):
            dq_ref[pl.ds(g * heads + h, here, stride=groups * heads), :] = dq[
                g * here : (g + 1) * here
            ]

    def step(keys):
        for h in range(heads):
            rescaled(h, scratch[2 * h], scratch[2 * h + 1], keys)
        for h in range(heads):
            gradients(h, scratch[2 * h], scratch[2 * h + 1], keys)

    half = pl.num_programs(0) // 2
    pl.when(i < half)(lambda: step(tokens + tokens // 2))
    pl.when(i >= half)(lambda: step(2 * tokens))

    @pl.when(i == pl.num_programs(0) - 1)
    def _():
        join_heads(dk, dv, (partner_ref, own_ref), tokens, heads, scale)


def pack(keys, values, heads):
    return pl.pallas_call(
        functools.partial(pack_kernel, heads),
        in_specs=[pl.BlockSpec(memory_space=pltpu.HBM)] * 2,
        out_specs=VMEM,
        out_shape=jax.ShapeDtypeStruct((2, *keys.shape), bf16),
        scratch_shapes=[
            pltpu.VMEM((2, *keys.shape), bf16),
            pltpu.VMEM((2, *keys.shape), f32),
            pltpu.SemaphoreType.DMA((2,)),
        ],
        compiler_params=params(True, 4),
        name="pack",
    )(keys, values)


def finish(own, crossed, arrived, heads):
    return pl.pallas_call(
        functools.partial(finish_kernel, heads),
        in_specs=[VMEM] * (3 + len(arrived)),
        out_specs=[VMEM] * 2,
        out_shape=[jax.ShapeDtypeStruct(own.shape[1:], f32)] * 2,
        compiler_params=params(True, 8),
        name="finish",
    )(own, *crossed, *arrived)


def whole(*shape):
    return pl.BlockSpec(shape, lambda i: (0,) * len(shape))


def stepped(kept, *shape):
    return VMEM if kept else pl.BlockSpec(shape, lambda i: (i, 0))


def across(kept, *shape):
    return VMEM if kept else pl.BlockSpec(shape, lambda i: (0, i))


def params(kept, megabytes=16):
    return pltpu.CompilerParams(vmem_limit_bytes=(megabytes if kept else 60) * 2**20)


def step_rows(kept, rows):
    if not kept:
        return 0
    return pl.multiple_of(pl.program_id(0) * rows, rows)


def prep(q, do, sizes):
    tokens, groups, heads, width, here, kept = sizes
    rows = tokens * groups * heads
    pieces = 4
    return pl.pallas_call(
        functools.partial(prep_kernel, sizes),
        in_specs=[pl.BlockSpec(memory_space=pltpu.HBM)] * 2,
        out_specs=[VMEM] * 2,
        out_shape=[jax.ShapeDtypeStruct((rows, width), bf16)] * 2,
        scratch_shapes=[
            pltpu.VMEM((2 * pieces, rows // pieces, width), f32),
            pltpu.VMEM((pieces, rows // pieces, width), bf16),
            pltpu.VMEM((pieces, rows // pieces, width), bf16),
            pltpu.SemaphoreType.DMA((pieces, 2)),
        ],
        compiler_params=params(kept),
        name="prep",
    )(q, do)


def near(qs, dos, start, own, partner, sizes):
    tokens, groups, heads, width, here, kept = sizes
    chunk = here * groups
    rows = tokens * groups * heads
    keys = 2 * tokens
    return pl.pallas_call(
        functools.partial(near_kernel, sizes),
        grid=(rows // (2 * chunk),),
        in_specs=[VMEM] * 5,
        out_specs=[
            stepped(kept, 2 * chunk, keys),
            stepped(kept, 2 * chunk, keys),
            whole(heads, keys, width),
            stepped(kept, 2 * chunk, 128),
            stepped(kept, 2 * chunk, 128),
            across(kept, width, 2 * chunk),
            across(kept, width, 2 * chunk),
        ],
        out_shape=[
            jax.ShapeDtypeStruct((rows, keys), bf16),
            jax.ShapeDtypeStruct((rows, keys), bf16),
            jax.ShapeDtypeStruct((heads, keys, width), bf16),
            jax.ShapeDtypeStruct((rows, 128), f32),
            jax.ShapeDtypeStruct((rows, 128), f32),
            jax.ShapeDtypeStruct((width, rows), bf16),
            jax.ShapeDtypeStruct((width, rows), bf16),
        ],
        scratch_shapes=[
            pltpu.VMEM((heads, keys, width), bf16),
            pltpu.VMEM((tokens, keys), f32),
        ]
        + [pltpu.VMEM((chunk, keys), f32)] * 4,
        compiler_params=params(kept),
        cost_estimate=pl.CostEstimate(
            flops=2 * 2 * rows * (keys) * width,
            bytes_accessed=8 * rows * (keys),
            transcendentals=rows * (keys),
        ),
        name="near",
    )(qs, dos, start, own, partner)


def far(start, log1, mean1, qs, dos, qt, dt, pairs, sizes):
    tokens, groups, heads, width, here, kept = sizes
    slots = len(pairs)
    chunk = here * groups
    rows = tokens * groups * heads
    keys = slots * tokens
    return pl.pallas_call(
        functools.partial(far_kernel, (tokens, groups, heads, slots, width, here, kept)),
        grid=(rows // (2 * chunk),),
        in_specs=[VMEM] + [stepped(kept, 2 * chunk, 128)] * 2 + [VMEM] * (4 + slots),
        out_specs=[
            whole(heads, keys, width),
            stepped(kept, 2 * chunk, keys),
            stepped(kept, 2 * chunk, 128),
            stepped(kept, 2 * chunk, 128),
        ]
        + [whole(2, tokens * heads, width)] * slots,
        out_shape=[
            jax.ShapeDtypeStruct((heads, keys, width), bf16),
            jax.ShapeDtypeStruct((rows, keys), bf16),
            jax.ShapeDtypeStruct((rows, 128), f32),
            jax.ShapeDtypeStruct((rows, 128), f32),
        ]
        + [jax.ShapeDtypeStruct((2, tokens * heads, width), bf16)] * slots,
        scratch_shapes=[
            pltpu.VMEM((heads, keys, width), bf16),
            pltpu.VMEM((tokens, keys), f32),
            pltpu.VMEM((heads, width, keys), f32),
            pltpu.VMEM((heads, width, keys), f32),
        ]
        + [pltpu.VMEM((chunk, keys), f32)] * 4
        + [pltpu.VMEM((groups * tokens if kept else 2 * chunk, keys), bf16)],
        compiler_params=params(kept),
        cost_estimate=pl.CostEstimate(
            flops=2 * 4 * rows * (keys) * width,
            bytes_accessed=8 * rows * (keys),
            transcendentals=rows * (keys),
        ),
        input_output_aliases={1: 2, 2: 3},
        name="far",
    )(start, log1, mean1, qs, dos, qt, dt, *pairs)


def ahead(k2, ds2):
    heads, _, width = k2.shape
    return pl.pallas_call(
        ahead_kernel,
        in_specs=[VMEM] * 2,
        out_specs=VMEM,
        out_shape=jax.ShapeDtypeStruct((ds2.shape[0] - ds2.shape[0] // (2 * heads), width), f32),
        compiler_params=params(True, 4),
        name="ahead",
    )(k2, ds2)


def tail(share, shift, k1, k2, qt, dt, w1, u1, ds2, early, sizes):
    tokens, groups, heads, width, here, kept = sizes
    chunk = here * groups
    rows = tokens * groups * heads
    blocks = tokens // here
    near_keys, far_keys = k1.shape[1], k2.shape[1]

    def both(columns):
        if kept:
            return VMEM
        return pl.BlockSpec((heads, chunk, columns), lambda i: (0, i, 0))

    def turned(h):
        if kept:
            return VMEM
        return pl.BlockSpec((width, chunk), lambda i: (0, h * blocks + i))

    def by_head(a):
        return a.reshape(heads, rows // heads, a.shape[1])

    return pl.pallas_call(
        functools.partial(tail_kernel, sizes),
        grid=(blocks,),
        in_specs=[
            whole(heads, near_keys, width),
            whole(heads, far_keys, width),
            both(128),
            both(128),
            both(near_keys),
            both(near_keys),
            both(far_keys),
        ]
        + [turned(h) for h in range(heads)] * 2
        + [VMEM] * len(early),
        out_specs=[pl.BlockSpec((chunk * heads, width), lambda i: (i, 0)), VMEM, VMEM],
        out_shape=[
            jax.ShapeDtypeStruct((rows, width), f32),
            jax.ShapeDtypeStruct((2, tokens * heads, width), f32),
            jax.ShapeDtypeStruct((2, tokens * heads, width), bf16),
        ],
        scratch_shapes=[
            pltpu.VMEM((heads, width, near_keys), f32),
            pltpu.VMEM((heads, width, near_keys), f32),
            *[pltpu.VMEM((chunk, near_keys), bf16)] * (2 * heads),
        ],
        compiler_params=params(kept, 14),
        cost_estimate=pl.CostEstimate(
            flops=6 * rows * (near_keys + far_keys) * width,
            bytes_accessed=8 * rows * (near_keys + far_keys),
            transcendentals=rows * (near_keys + far_keys),
        ),
        name="tail",
    )(
        k1,
        k2,
        *[by_head(a) for a in (share, shift, w1, u1, ds2)],
        *[qt] * heads,
        *[dt] * heads,
        *early,
    )


def shards(queries, keys, values, output_gradient, band_start):
    tokens, heads, groups, width = queries.shape
    count = lax.axis_size("ctx")
    reach = min(WINDOW // tokens, count - 1)
    hops = min((reach + 1) // 2, count // 2 - 1)

    def in_hbm(a):
        return pltpu.with_memory_space_constraint(a, pltpu.HBM)

    own = pack(
        in_hbm(keys.reshape(tokens * heads, width)),
        in_hbm(values.reshape(tokens * heads, width)),
        heads,
    )
    same = [moved(own, 2 * d) for d in range(1, hops + 1)]
    partner = swapped(own)
    start = band_start.reshape(1, tokens)
    kept = hops <= 2
    here = tokens // (4 if kept else 8)
    sizes = (tokens, groups, heads, width, here, kept)

    def flat(a):
        return a.transpose(0, 2, 1, 3).reshape(tokens * groups * heads, width)

    qs, dos = prep(in_hbm(flat(queries)), in_hbm(flat(output_gradient)), sizes)
    w1, u1, k1, log1, mean1, qt, dt = near(qs, dos, start, own, partner, sizes)
    *same, log1 = lax.optimization_barrier((*same, log1))
    other = [swapped(block) for block in same]
    k2, ds2, share, shift, *parts = far(
        start, log1, mean1, qs, dos, qt, dt, same + other, sizes
    )
    early = [ahead(k2, ds2)] if kept else []
    arriving = []
    for d in range(hops):
        crossed = swapped(parts[hops + d])
        both = (parts[d].astype(f32) + crossed.astype(f32)).astype(bf16)
        both, share, early = lax.optimization_barrier((both, share, early))
        arriving.append(moved(both, -2 * (d + 1)))
    dq, total, crossing = tail(
        share, shift, k1, k2, qt, dt, w1, u1, ds2, early, sizes
    )
    crossed = [swapped(half) for half in crossing]
    dk, dv = finish(total, crossed, arriving, heads)
    return (
        dq.reshape(tokens, groups, heads, width).transpose(0, 2, 1, 3),
        dk.reshape(tokens, heads, width),
        dv.reshape(tokens, heads, width),
    )


def solution(mesh):
    rows = P(("rep", "ctx"), "kv", None, None)
    keys = P(("rep", "ctx"), "kv", None)
    return jax.shard_map(
        shards,
        mesh=mesh,
        in_specs=(rows, keys, keys, rows, P(("rep", "ctx"))),
        out_specs=(rows, keys, keys),
        check_vma=False,
    )
```

```python
import functools

import jax
import jax.numpy as jnp
from jax import lax
from jax.experimental import pallas as pl
from jax.experimental.pallas import tpu as pltpu
from jax.sharding import PartitionSpec as P

WINDOW = 2048
LOG2E = 1.4426950408889634
MASKED = -1e30
f32 = jnp.float32
bf16 = jnp.bfloat16
ACROSS = (((1,), (1,)), ((), ()))
VMEM = pl.BlockSpec(memory_space=pltpu.VMEM)


def moved(block, distance):
    devices = range(lax.axis_size("ctx"))
    route = [(i - distance, i) for i in devices if i - distance in devices]
    return lax.ppermute(block, "ctx", route)


def swapped(block):
    return lax.ppermute(block, "ctx", [(i, i ^ 1) for i in range(lax.axis_size("ctx"))])


def split_heads(pair_refs, k_s, v_s, tokens, heads):
    for slot, pair in enumerate(pair_refs):
        for h in range(heads):
            rows = slice(h * tokens, (h + 1) * tokens)
            k_s[h, slot * tokens : (slot + 1) * tokens, :] = pair[0, rows, :]
            v_s[h, slot * tokens : (slot + 1) * tokens, :] = pair[1, rows, :]


def join_heads(dk, dv, part_refs, tokens, heads, scale):
    for source, grad in ((0, dk), (1, dv)):
        for slot, part in enumerate(part_refs):
            for h in range(heads):
                block = grad[h, :, slot * tokens : (slot + 1) * tokens].T
                if source == 0:
                    block *= scale
                part[source, h * tokens : (h + 1) * tokens, :] = block.astype(part.dtype)


def pack_kernel(heads, k_ref, v_ref, pair_ref, narrow, wide, arrived):
    tokens = k_ref.shape[0] // heads
    loads = [
        pltpu.make_async_copy(ref, narrow.at[source], arrived.at[source])
        for source, ref in ((0, k_ref), (1, v_ref))
    ]
    for load in loads:
        load.start()
    for source in range(2):
        loads[source].wait()
        wide[source] = narrow[source].astype(f32)
        for h in range(heads):
            pair_ref[source, h * tokens : (h + 1) * tokens, :] = wide[
                source, pl.ds(h, tokens, stride=heads), :
            ].astype(bf16)


def finish_kernel(heads, own_ref, crossed_k_ref, crossed_v_ref, *refs):
    tokens = own_ref.shape[1] // heads
    for source, crossed in ((0, crossed_k_ref), (1, crossed_v_ref)):
        for h in range(heads):
            rows = slice(h * tokens, (h + 1) * tokens)
            total = own_ref[source, rows, :] + crossed[rows, :].astype(f32)
            for arrived in refs[:-2]:
                total += arrived[source, rows, :].astype(f32)
            refs[source - 2][pl.ds(h, tokens, stride=heads), :] = total


def fill_bias(bias, start_ref, first_keys, tokens):
    down = lax.broadcasted_iota(jnp.int32, (tokens, tokens), 0)
    along = lax.broadcasted_iota(jnp.int32, (tokens, tokens), 1)
    start = jnp.sum(
        jnp.where(down == along, start_ref[...].astype(f32), 0.0), -1, keepdims=True
    ).astype(jnp.int32)
    row = lax.axis_index("ctx") * tokens + lax.broadcasted_iota(jnp.int32, (tokens, 1), 0)
    for slot, first in enumerate(first_keys):
        key = first + lax.broadcasted_iota(jnp.int32, (1, tokens), 1)
        bias[:, slot * tokens : (slot + 1) * tokens] = jnp.where(
            (key <= row) & (key >= start), 0.0, MASKED
        )


def spread(lanes, width):
    return jnp.concatenate([lanes] * (width // lanes.shape[1]), 1)


def prep_kernel(sizes, q_ref, do_ref, qs_ref, dos_ref, wide, q_in, do_in, arrived):
    tokens, groups, heads, width, here, kept = sizes
    pieces = q_in.shape[0]
    size = tokens // pieces * groups * heads
    blocks = tokens // here
    loads = []
    for n in range(pieces):
        for k, (source, target) in enumerate(((q_ref, q_in), (do_ref, do_in))):
            load = pltpu.make_async_copy(
                source.at[pl.ds(n * size, size), :], target.at[n], arrived.at[n, k]
            )
            load.start()
            loads.append(load)
    for n in range(pieces):
        for k, (source, split) in enumerate(((q_in, qs_ref), (do_in, dos_ref))):
            loads[2 * n + k].wait()
            wide[2 * n + k] = source[n].astype(f32)
            for h in range(heads):
                for b in range(blocks // pieces):
                    for g in range(groups):
                        at = ((h * blocks + n * (blocks // pieces) + b) * groups + g) * here
                        begin = (b * here * groups + g) * heads + h
                        split[at : at + here, :] = wide[
                            2 * n + k, pl.ds(begin, here, stride=groups * heads), :
                        ].astype(bf16)


def near_kernel(
    sizes, qs, dos, start_ref, own_ref, partner_ref,
    w_ref, u_ref, k_ref, log_ref, mean_ref, qt_ref, dot_ref,
    v_s, bias, s_a, d_a, s_b, d_b,
):
    tokens, groups, heads, width, here, kept = sizes
    chunk = here * groups
    blocks = tokens // here
    chunks = blocks * heads
    i = pl.program_id(0)
    first = step_rows(kept, 2 * chunk)
    slope = width**-0.5 * LOG2E
    lower, every = tokens + tokens // 2, 2 * tokens
    early = i % (blocks // 2) < blocks // 4

    def products(c, s, d, keys):
        rows = pl.ds(pl.multiple_of(c * chunk, chunk), chunk)
        h = c // blocks
        s[:, :keys] = lax.dot_general(qs[rows, :], k_ref[h, :keys], ACROSS, preferred_element_type=f32)
        d[:, :keys] = lax.dot_general(dos[rows, :], v_s[h, :keys], ACROSS, preferred_element_type=f32)

    def weights(c, half, s, d, keys):
        size = chunk // 3
        band = bias[pl.ds(pl.multiple_of(c % blocks * here, here), here), :keys]
        band = jnp.concatenate([band] * (size // here), 0)
        for row in range(0, chunk, size):
            rows = slice(row, row + size)
            out = pl.ds(first + half * chunk + row, size)
            x = s[rows, :keys] * slope + band
            dp = d[rows, :keys]
            m = jnp.max(x, -1, keepdims=True)
            p = jnp.exp2(x - m)
            total = jnp.sum(p, -1, keepdims=True)
            inverse = 1.0 / total
            dot = jnp.sum(p * dp, -1, keepdims=True) * inverse
            w = p * inverse
            w_ref[out, :keys] = w.astype(bf16)
            u_ref[out, :keys] = (w * (dp - dot)).astype(bf16)
            log_ref[out, :] = jnp.broadcast_to(m + jnp.log2(total), (size, 128))
            mean_ref[out, :] = jnp.broadcast_to(dot, (size, 128))

    @pl.when(i == 0)
    def _():
        split_heads((partner_ref, own_ref), k_ref, v_s, tokens, heads)
        ctx = lax.axis_index("ctx")
        fill_bias(bias, start_ref, ((ctx + 1 - 2 * (ctx % 2)) * tokens, ctx * tokens), tokens)
        products(0, s_a, d_a, lower)

    both = pl.ds(pl.multiple_of(i * 2 * chunk, 2 * chunk), 2 * chunk)
    columns = pl.ds(first, 2 * chunk)

    def step(keys, next_keys):
        products(2 * i + 1, s_b, d_b, keys)
        qt_ref[:, columns] = qs[both, :].T
        weights(2 * i, 0, s_a, d_a, keys)
        products(jnp.minimum(2 * i + 2, chunks - 1), s_a, d_a, next_keys)
        dot_ref[:, columns] = dos[both, :].T
        weights(2 * i + 1, 1, s_b, d_b, keys)

    @pl.when(early)
    def _():
        step(lower, every)

    @pl.when(jnp.logical_not(early))
    def _():
        step(every, lower if blocks == 4 else every)


def far_kernel(
    sizes, start_ref, log1_ref, mean1_ref, qs_ref, dos_ref, qt_ref, dot_ref, *refs,
):
    tokens, groups, heads, slots, width, here, kept = sizes
    pair_refs = refs[:slots]
    k_ref, ds_ref, share_ref, shift_ref = refs[slots : slots + 4]
    part_refs = refs[slots + 4 : 2 * slots + 4]
    v_s, bias, dk, dv, s_a, d_a, s_b, d_b, w_s = refs[2 * slots + 4 :]
    chunk = here * groups
    blocks = tokens // here
    chunks = blocks * heads
    hops = slots // 2
    i = pl.program_id(0)
    first = step_rows(kept, 2 * chunk)
    slope = width**-0.5 * LOG2E
    ctx = lax.axis_index("ctx")
    reached = ctx >= 2
    steps = blocks // 2

    def products(c, s, d):
        rows = pl.ds(pl.multiple_of(c * chunk, chunk), chunk)
        h = c // blocks
        s[...] = lax.dot_general(qs_ref[rows, :], k_ref[h], ACROSS, preferred_element_type=f32)
        d[...] = lax.dot_general(dos_ref[rows, :], v_s[h], ACROSS, preferred_element_type=f32)

    def head_gradients(h):
        rows = slice(h * groups * tokens, (h + 1) * groups * tokens)
        grads = (
            jnp.dot(qt_ref[:, rows], ds_ref[rows, :], preferred_element_type=f32) * width**-0.5,
            jnp.dot(dot_ref[:, rows], w_s[rows, :], preferred_element_type=f32),
        )
        for source, grad in enumerate(grads):
            for slot, part in enumerate(part_refs):
                part[source, h * tokens : (h + 1) * tokens, :] = grad[
                    :, slot * tokens : (slot + 1) * tokens
                ].T.astype(bf16)

    def step_gradients():
        h = i // steps
        rows = pl.ds(pl.multiple_of(i * 2 * chunk, 2 * chunk), 2 * chunk)
        dk[h] += jnp.dot(qt_ref[:, rows], ds_ref[...], preferred_element_type=f32)
        dv[h] += jnp.dot(dot_ref[:, rows], w_s[...], preferred_element_type=f32)

    def weights(c, half, s, d, first):
        size = chunk // 3
        band = bias[pl.ds(pl.multiple_of(c % blocks * here, here), here), :]
        band = jnp.concatenate([band] * (size // here), 0)
        for row in range(0, chunk, size):
            rows = slice(row, row + size)
            out = pl.ds(first + half * chunk + row, size)
            log1 = log1_ref[out, :]
            mean1 = mean1_ref[out, :]
            x = s[rows, :] * slope + band
            dp = d[rows, :]
            m = jnp.maximum(jnp.max(x, -1, keepdims=True), log1)
            p = jnp.exp2(x - spread(m, x.shape[1]))
            before = jnp.exp2(log1 - m)
            inverse = 1.0 / (jnp.sum(p, -1, keepdims=True) + before)
            mean = (jnp.sum(p * dp, -1, keepdims=True) + before * mean1) * inverse
            w = p * spread(inverse, x.shape[1])
            ds = (w * (dp - spread(mean, x.shape[1]))).astype(bf16)
            there = out if kept else pl.ds(half * chunk + row, size)
            w_s[there, :] = w.astype(bf16)
            ds_ref[out, :] = ds
            share_ref[out, :] = before * inverse
            shift_ref[out, :] = mean1 - mean

    @pl.when(reached & (i == 0))
    def _():
        split_heads(pair_refs, k_ref, v_s, tokens, heads)
        partner = ctx + 1 - 2 * (ctx % 2)
        starts = [(ctx - 2 * d) * tokens for d in range(1, hops + 1)]
        starts += [(partner - 2 * d) * tokens for d in range(1, hops + 1)]
        fill_bias(bias, start_ref, starts, tokens)
        if not kept:
            dk[...] = jnp.zeros_like(dk)
            dv[...] = jnp.zeros_like(dv)
        products(0, s_a, d_a)

    def step(i, first):
        products(2 * i + 1, s_b, d_b)
        weights(2 * i, 0, s_a, d_a, first)
        products(jnp.minimum(2 * i + 2, chunks - 1), s_a, d_a)
        weights(2 * i + 1, 1, s_b, d_b, first)

    if kept:
        ends = [steps * h for h in range(1, heads)]
        plain = reached
        for end in ends:
            plain &= i != end

        @pl.when(plain)
        def _():
            step(i, first)

        for h, end in enumerate(ends):

            @pl.when(reached & (i == end))
            def _():
                head_gradients(h)
                step(end, end * 2 * chunk)

        @pl.when(reached & (i == pl.num_programs(0) - 1))
        def _():
            head_gradients(heads - 1)
    else:

        @pl.when(reached)
        def _():
            step(i, first)
            step_gradients()

        @pl.when(reached & (i == pl.num_programs(0) - 1))
        def _():
            join_heads(dk, dv, part_refs, tokens, heads, width**-0.5)

    @pl.when(jnp.logical_not(reached))
    def _():
        these = pl.ds(first, 2 * chunk)
        ds_ref[these, :] = jnp.zeros((2 * chunk, ds_ref.shape[1]), bf16)
        share_ref[these, :] = jnp.ones((2 * chunk, 128), f32)
        shift_ref[these, :] = jnp.zeros((2 * chunk, 128), f32)

    @pl.when(jnp.logical_not(reached) & (i == 0))
    def _():
        k_ref[...] = jnp.zeros_like(k_ref)
        for part in part_refs:
            part[...] = jnp.zeros_like(part)


def ahead_kernel(k_ref, ds_ref, dq_ref):
    heads = k_ref.shape[0]
    each = ds_ref.shape[0] // heads
    for h in range(heads):
        rows = slice(h * each, h * each + (each if h < heads - 1 else each // 2))
        dq_ref[rows, :] = jnp.dot(ds_ref[rows, :], k_ref[h], preferred_element_type=f32)


def tail_kernel(
    sizes, k1_ref, k2_ref, share_ref, shift_ref, w1_ref, u1_ref, ds2_ref, *refs,
):
    tokens, groups, heads, width, here, kept = sizes
    qt_refs, dot_refs = refs[:heads], refs[heads : 2 * heads]
    ahead_ref = refs[2 * heads]
    dq_ref, own_ref, partner_ref, dk, dv, *scratch = refs[2 * heads + (1 if kept else 0) :]
    chunk = here * groups
    i = pl.program_id(0)
    scale = width**-0.5
    first = step_rows(kept, chunk)

    @pl.when(i == 0)
    def _():
        dk[...] = jnp.zeros_like(dk)
        dv[...] = jnp.zeros_like(dv)

    def rescaled(h, w_s, ds_s, keys):
        size = 64 if chunk % 64 == 0 else chunk
        for row in range(0, chunk, size):
            rows = pl.ds(first + row, size)
            w = w1_ref[h, rows, :keys].astype(f32)
            share = spread(share_ref[h, rows, :], w.shape[1])
            shift = spread(shift_ref[h, rows, :], w.shape[1])
            w_s[row : row + size, :keys] = (w * share).astype(bf16)
            ds_s[row : row + size, :keys] = (
                (u1_ref[h, rows, :keys].astype(f32) + w * shift) * share
            ).astype(bf16)

    def gradients(h, w_s, ds_s, keys):
        columns = pl.ds((h * tokens * groups if kept else 0) + first, chunk)
        ds = ds_s[:, :keys]
        dk[h, :, :keys] += jnp.dot(qt_refs[h][:, columns], ds, preferred_element_type=f32)
        dv[h, :, :keys] += jnp.dot(
            dot_refs[h][:, columns], w_s[:, :keys], preferred_element_type=f32
        )
        dq = jnp.dot(ds, k1_ref[h, :keys], preferred_element_type=f32)
        if kept and (h < heads - 1 or keys < 2 * tokens):
            dq += ahead_ref[pl.ds(h * groups * tokens + first, chunk), :]
        else:
            dq += jnp.dot(
                ds2_ref[h, pl.ds(first, chunk), :], k2_ref[h], preferred_element_type=f32
            )
        dq *= scale
        for g in range(groups):
            dq_ref[pl.ds(g * heads + h, here, stride=groups * heads), :] = dq[
                g * here : (g + 1) * here
            ]

    def step(keys):
        for h in range(heads):
            rescaled(h, scratch[2 * h], scratch[2 * h + 1], keys)
        for h in range(heads):
            gradients(h, scratch[2 * h], scratch[2 * h + 1], keys)

    half = pl.num_programs(0) // 2
    pl.when(i < half)(lambda: step(tokens + tokens // 2))
    pl.when(i >= half)(lambda: step(2 * tokens))

    @pl.when(i == pl.num_programs(0) - 1)
    def _():
        join_heads(dk, dv, (partner_ref, own_ref), tokens, heads, scale)


def pack(keys, values, heads):
    return pl.pallas_call(
        functools.partial(pack_kernel, heads),
        in_specs=[pl.BlockSpec(memory_space=pltpu.HBM)] * 2,
        out_specs=VMEM,
        out_shape=jax.ShapeDtypeStruct((2, *keys.shape), bf16),
        scratch_shapes=[
            pltpu.VMEM((2, *keys.shape), bf16),
            pltpu.VMEM((2, *keys.shape), f32),
            pltpu.SemaphoreType.DMA((2,)),
        ],
        compiler_params=params(True, 4),
        name="pack",
    )(keys, values)


def finish(own, crossed, arrived, heads):
    return pl.pallas_call(
        functools.partial(finish_kernel, heads),
        in_specs=[VMEM] * (3 + len(arrived)),
        out_specs=[VMEM] * 2,
        out_shape=[jax.ShapeDtypeStruct(own.shape[1:], f32)] * 2,
        compiler_params=params(True, 8),
        name="finish",
    )(own, *crossed, *arrived)


def whole(*shape):
    return pl.BlockSpec(shape, lambda i: (0,) * len(shape))


def stepped(kept, *shape):
    return VMEM if kept else pl.BlockSpec(shape, lambda i: (i, 0))


def across(kept, *shape):
    return VMEM if kept else pl.BlockSpec(shape, lambda i: (0, i))


def params(kept, megabytes=16):
    return pltpu.CompilerParams(vmem_limit_bytes=(megabytes if kept else 60) * 2**20)


def step_rows(kept, rows):
    if not kept:
        return 0
    return pl.multiple_of(pl.program_id(0) * rows, rows)


def prep(q, do, sizes):
    tokens, groups, heads, width, here, kept = sizes
    rows = tokens * groups * heads
    pieces = 4
    return pl.pallas_call(
        functools.partial(prep_kernel, sizes),
        in_specs=[pl.BlockSpec(memory_space=pltpu.HBM)] * 2,
        out_specs=[VMEM] * 2,
        out_shape=[jax.ShapeDtypeStruct((rows, width), bf16)] * 2,
        scratch_shapes=[
            pltpu.VMEM((2 * pieces, rows // pieces, width), f32),
            pltpu.VMEM((pieces, rows // pieces, width), bf16),
            pltpu.VMEM((pieces, rows // pieces, width), bf16),
            pltpu.SemaphoreType.DMA((pieces, 2)),
        ],
        compiler_params=params(kept, 12),
        name="prep",
    )(q, do)


def near(qs, dos, start, own, partner, sizes):
    tokens, groups, heads, width, here, kept = sizes
    chunk = here * groups
    rows = tokens * groups * heads
    keys = 2 * tokens
    return pl.pallas_call(
        functools.partial(near_kernel, sizes),
        grid=(rows // (2 * chunk),),
        in_specs=[VMEM] * 5,
        out_specs=[
            stepped(kept, 2 * chunk, keys),
            stepped(kept, 2 * chunk, keys),
            whole(heads, keys, width),
            stepped(kept, 2 * chunk, 128),
            stepped(kept, 2 * chunk, 128),
            across(kept, width, 2 * chunk),
            across(kept, width, 2 * chunk),
        ],
        out_shape=[
            jax.ShapeDtypeStruct((rows, keys), bf16),
            jax.ShapeDtypeStruct((rows, keys), bf16),
            jax.ShapeDtypeStruct((heads, keys, width), bf16),
            jax.ShapeDtypeStruct((rows, 128), f32),
            jax.ShapeDtypeStruct((rows, 128), f32),
            jax.ShapeDtypeStruct((width, rows), bf16),
            jax.ShapeDtypeStruct((width, rows), bf16),
        ],
        scratch_shapes=[
            pltpu.VMEM((heads, keys, width), bf16),
            pltpu.VMEM((tokens, keys), f32),
        ]
        + [pltpu.VMEM((chunk, keys), f32)] * 4,
        compiler_params=params(kept, 12),
        cost_estimate=pl.CostEstimate(
            flops=2 * 2 * rows * (keys) * width,
            bytes_accessed=8 * rows * (keys),
            transcendentals=rows * (keys),
        ),
        name="near",
    )(qs, dos, start, own, partner)


def far(start, log1, mean1, qs, dos, qt, dt, pairs, sizes):
    tokens, groups, heads, width, here, kept = sizes
    slots = len(pairs)
    chunk = here * groups
    rows = tokens * groups * heads
    keys = slots * tokens
    return pl.pallas_call(
        functools.partial(far_kernel, (tokens, groups, heads, slots, width, here, kept)),
        grid=(rows // (2 * chunk),),
        in_specs=[VMEM] + [stepped(kept, 2 * chunk, 128)] * 2 + [VMEM] * (4 + slots),
        out_specs=[
            whole(heads, keys, width),
            stepped(kept, 2 * chunk, keys),
            stepped(kept, 2 * chunk, 128),
            stepped(kept, 2 * chunk, 128),
        ]
        + [whole(2, tokens * heads, width)] * slots,
        out_shape=[
            jax.ShapeDtypeStruct((heads, keys, width), bf16),
            jax.ShapeDtypeStruct((rows, keys), bf16),
            jax.ShapeDtypeStruct((rows, 128), f32),
            jax.ShapeDtypeStruct((rows, 128), f32),
        ]
        + [jax.ShapeDtypeStruct((2, tokens * heads, width), bf16)] * slots,
        scratch_shapes=[
            pltpu.VMEM((heads, keys, width), bf16),
            pltpu.VMEM((tokens, keys), f32),
            pltpu.VMEM((heads, width, keys), f32),
            pltpu.VMEM((heads, width, keys), f32),
        ]
        + [pltpu.VMEM((chunk, keys), f32)] * 4
        + [pltpu.VMEM((rows if kept else 2 * chunk, keys), bf16)],
        compiler_params=params(kept, 16),
        cost_estimate=pl.CostEstimate(
            flops=2 * 4 * rows * (keys) * width,
            bytes_accessed=8 * rows * (keys),
            transcendentals=rows * (keys),
        ),
        input_output_aliases={1: 2, 2: 3},
        name="far",
    )(start, log1, mean1, qs, dos, qt, dt, *pairs)


def ahead(k2, ds2):
    heads, _, width = k2.shape
    return pl.pallas_call(
        ahead_kernel,
        in_specs=[VMEM] * 2,
        out_specs=VMEM,
        out_shape=jax.ShapeDtypeStruct((ds2.shape[0] - ds2.shape[0] // (2 * heads), width), f32),
        compiler_params=params(True, 4),
        name="ahead",
    )(k2, ds2)


def tail(share, shift, k1, k2, qt, dt, w1, u1, ds2, early, sizes):
    tokens, groups, heads, width, here, kept = sizes
    chunk = here * groups
    rows = tokens * groups * heads
    blocks = tokens // here
    near_keys, far_keys = k1.shape[1], k2.shape[1]

    def both(columns):
        if kept:
            return VMEM
        return pl.BlockSpec((heads, chunk, columns), lambda i: (0, i, 0))

    def turned(h):
        if kept:
            return VMEM
        return pl.BlockSpec((width, chunk), lambda i: (0, h * blocks + i))

    def by_head(a):
        return a.reshape(heads, rows // heads, a.shape[1])

    return pl.pallas_call(
        functools.partial(tail_kernel, sizes),
        grid=(blocks,),
        in_specs=[
            whole(heads, near_keys, width),
            whole(heads, far_keys, width),
            both(128),
            both(128),
            both(near_keys),
            both(near_keys),
            both(far_keys),
        ]
        + [turned(h) for h in range(heads)] * 2
        + [VMEM] * len(early),
        out_specs=[pl.BlockSpec((chunk * heads, width), lambda i: (i, 0)), VMEM, VMEM],
        out_shape=[
            jax.ShapeDtypeStruct((rows, width), f32),
            jax.ShapeDtypeStruct((2, tokens * heads, width), f32),
            jax.ShapeDtypeStruct((2, tokens * heads, width), bf16),
        ],
        scratch_shapes=[
            pltpu.VMEM((heads, width, near_keys), f32),
            pltpu.VMEM((heads, width, near_keys), f32),
            *[pltpu.VMEM((chunk, near_keys), bf16)] * (2 * heads),
        ],
        compiler_params=params(kept, 12),
        cost_estimate=pl.CostEstimate(
            flops=6 * rows * (near_keys + far_keys) * width,
            bytes_accessed=8 * rows * (near_keys + far_keys),
            transcendentals=rows * (near_keys + far_keys),
        ),
        name="tail",
    )(
        k1,
        k2,
        *[by_head(a) for a in (share, shift, w1, u1, ds2)],
        *[qt] * heads,
        *[dt] * heads,
        *early,
    )


def shards(queries, keys, values, output_gradient, band_start):
    tokens, heads, groups, width = queries.shape
    count = lax.axis_size("ctx")
    reach = min(WINDOW // tokens, count - 1)
    hops = min((reach + 1) // 2, count // 2 - 1)

    def in_hbm(a):
        return pltpu.with_memory_space_constraint(a, pltpu.HBM)

    own = pack(
        in_hbm(keys.reshape(tokens * heads, width)),
        in_hbm(values.reshape(tokens * heads, width)),
        heads,
    )
    same = [moved(own, 2 * d) for d in range(1, hops + 1)]
    partner = swapped(own)
    start = band_start.reshape(1, tokens)
    kept = hops <= 2
    here = tokens // (4 if kept else 8)
    sizes = (tokens, groups, heads, width, here, kept)

    def flat(a):
        return a.transpose(0, 2, 1, 3).reshape(tokens * groups * heads, width)

    qs, dos = prep(in_hbm(flat(queries)), in_hbm(flat(output_gradient)), sizes)
    w1, u1, k1, log1, mean1, qt, dt = near(qs, dos, start, own, partner, sizes)
    *same, log1 = lax.optimization_barrier((*same, log1))
    other = [swapped(block) for block in same]
    k2, ds2, share, shift, *parts = far(
        start, log1, mean1, qs, dos, qt, dt, same + other, sizes
    )
    early = [ahead(k2, ds2)] if kept else []
    arriving = []
    for d in range(hops):
        crossed = swapped(parts[hops + d])
        both = (parts[d].astype(f32) + crossed.astype(f32)).astype(bf16)
        both, share, early = lax.optimization_barrier((both, share, early))
        arriving.append(moved(both, -2 * (d + 1)))
    dq, total, crossing = tail(
        share, shift, k1, k2, qt, dt, w1, u1, ds2, early, sizes
    )
    crossed = [swapped(half) for half in crossing]
    dk, dv = finish(total, crossed, arriving, heads)
    return (
        dq.reshape(tokens, groups, heads, width).transpose(0, 2, 1, 3),
        dk.reshape(tokens, heads, width),
        dv.reshape(tokens, heads, width),
    )


def solution(mesh):
    rows = P(("rep", "ctx"), "kv", None, None)
    keys = P(("rep", "ctx"), "kv", None)
    return jax.shard_map(
        shards,
        mesh=mesh,
        in_specs=(rows, keys, keys, rows, P(("rep", "ctx"))),
        out_specs=(rows, keys, keys),
        check_vma=False,
    )
```

```python
import functools

import jax
import jax.numpy as jnp
from jax import lax
from jax.experimental import pallas as pl
from jax.experimental.pallas import tpu as pltpu
from jax.sharding import PartitionSpec as P

WINDOW = 2048
LOG2E = 1.4426950408889634
MASKED = -1e30
f32 = jnp.float32
bf16 = jnp.bfloat16
ACROSS = (((1,), (1,)), ((), ()))
VMEM = pl.BlockSpec(memory_space=pltpu.VMEM)


def moved(block, distance):
    devices = range(lax.axis_size("ctx"))
    route = [(i - distance, i) for i in devices if i - distance in devices]
    return lax.ppermute(block, "ctx", route)


def swapped(block):
    return lax.ppermute(block, "ctx", [(i, i ^ 1) for i in range(lax.axis_size("ctx"))])


def split_heads(pair_refs, k_s, v_s, tokens, heads):
    for slot, pair in enumerate(pair_refs):
        for h in range(heads):
            rows = slice(h * tokens, (h + 1) * tokens)
            k_s[h, slot * tokens : (slot + 1) * tokens, :] = pair[0, rows, :]
            v_s[h, slot * tokens : (slot + 1) * tokens, :] = pair[1, rows, :]


def join_heads(dk, dv, part_refs, tokens, heads, scale):
    for source, grad in ((0, dk), (1, dv)):
        for slot, part in enumerate(part_refs):
            for h in range(heads):
                block = grad[h, :, slot * tokens : (slot + 1) * tokens].T
                if source == 0:
                    block *= scale
                part[source, h * tokens : (h + 1) * tokens, :] = block.astype(part.dtype)


def pack_kernel(heads, k_ref, v_ref, pair_ref, narrow, wide, arrived):
    tokens = k_ref.shape[0] // heads
    loads = [
        pltpu.make_async_copy(ref, narrow.at[source], arrived.at[source])
        for source, ref in ((0, k_ref), (1, v_ref))
    ]
    for load in loads:
        load.start()
    for source in range(2):
        loads[source].wait()
        wide[source] = narrow[source].astype(f32)
        for h in range(heads):
            pair_ref[source, h * tokens : (h + 1) * tokens, :] = wide[
                source, pl.ds(h, tokens, stride=heads), :
            ].astype(bf16)


def finish_kernel(heads, own_ref, crossed_k_ref, crossed_v_ref, *refs):
    tokens = own_ref.shape[1] // heads
    for source, crossed in ((0, crossed_k_ref), (1, crossed_v_ref)):
        for h in range(heads):
            rows = slice(h * tokens, (h + 1) * tokens)
            total = own_ref[source, rows, :] + crossed[rows, :].astype(f32)
            for arrived in refs[:-2]:
                total += arrived[source, rows, :].astype(f32)
            refs[source - 2][pl.ds(h, tokens, stride=heads), :] = total


def fill_bias(bias, start_ref, first_keys, tokens):
    down = lax.broadcasted_iota(jnp.int32, (tokens, tokens), 0)
    along = lax.broadcasted_iota(jnp.int32, (tokens, tokens), 1)
    start = jnp.sum(
        jnp.where(down == along, start_ref[...].astype(f32), 0.0), -1, keepdims=True
    ).astype(jnp.int32)
    row = lax.axis_index("ctx") * tokens + lax.broadcasted_iota(jnp.int32, (tokens, 1), 0)
    for slot, first in enumerate(first_keys):
        key = first + lax.broadcasted_iota(jnp.int32, (1, tokens), 1)
        bias[:, slot * tokens : (slot + 1) * tokens] = jnp.where(
            (key <= row) & (key >= start), 0.0, MASKED
        )


def spread(lanes, width):
    return jnp.concatenate([lanes] * (width // lanes.shape[1]), 1)


def prep_kernel(sizes, q_ref, do_ref, qs_ref, dos_ref, wide, q_in, do_in, arrived):
    tokens, groups, heads, width, here, kept = sizes
    pieces = q_in.shape[0]
    size = tokens // pieces * groups * heads
    blocks = tokens // here
    loads = []
    for n in range(pieces):
        for k, (source, target) in enumerate(((q_ref, q_in), (do_ref, do_in))):
            load = pltpu.make_async_copy(
                source.at[pl.ds(n * size, size), :], target.at[n], arrived.at[n, k]
            )
            load.start()
            loads.append(load)
    for n in range(pieces):
        for k, (source, split) in enumerate(((q_in, qs_ref), (do_in, dos_ref))):
            loads[2 * n + k].wait()
            wide[2 * n + k] = source[n].astype(f32)
            for h in range(heads):
                for b in range(blocks // pieces):
                    for g in range(groups):
                        at = ((h * blocks + n * (blocks // pieces) + b) * groups + g) * here
                        begin = (b * here * groups + g) * heads + h
                        split[at : at + here, :] = wide[
                            2 * n + k, pl.ds(begin, here, stride=groups * heads), :
                        ].astype(bf16)


def near_kernel(
    sizes, qs, dos, start_ref, own_ref, partner_ref,
    w_ref, u_ref, k_ref, log_ref, mean_ref, qt_ref, dot_ref,
    v_s, bias, s_a, d_a, s_b, d_b,
):
    tokens, groups, heads, width, here, kept = sizes
    chunk = here * groups
    blocks = tokens // here
    chunks = blocks * heads
    i = pl.program_id(0)
    first = step_rows(kept, 2 * chunk)
    slope = width**-0.5 * LOG2E
    lower, every = tokens + tokens // 2, 2 * tokens
    early = i % (blocks // 2) < blocks // 4

    def products(c, s, d, keys):
        rows = pl.ds(pl.multiple_of(c * chunk, chunk), chunk)
        h = c // blocks
        s[:, :keys] = lax.dot_general(qs[rows, :], k_ref[h, :keys], ACROSS, preferred_element_type=f32)
        d[:, :keys] = lax.dot_general(dos[rows, :], v_s[h, :keys], ACROSS, preferred_element_type=f32)

    def weights(c, half, s, d, keys):
        size = chunk // (2 if kept else 3)
        band = bias[pl.ds(pl.multiple_of(c % blocks * here, here), here), :keys]
        band = jnp.concatenate([band] * (size // here), 0)
        for row in range(0, chunk, size):
            rows = slice(row, row + size)
            out = pl.ds(first + half * chunk + row, size)
            x = s[rows, :keys] * slope + band
            dp = d[rows, :keys]
            m = jnp.max(x, -1, keepdims=True)
            p = jnp.exp2(x - m)
            total = jnp.sum(p, -1, keepdims=True)
            inverse = 1.0 / total
            dot = jnp.sum(p * dp, -1, keepdims=True) * inverse
            w = p * inverse
            w_ref[out, :keys] = w.astype(bf16)
            u_ref[out, :keys] = (w * (dp - dot)).astype(bf16)
            log_ref[out, :] = jnp.broadcast_to(m + jnp.log2(total), (size, 128))
            mean_ref[out, :] = jnp.broadcast_to(dot, (size, 128))

    @pl.when(i == 0)
    def _():
        split_heads((partner_ref, own_ref), k_ref, v_s, tokens, heads)
        ctx = lax.axis_index("ctx")
        fill_bias(bias, start_ref, ((ctx + 1 - 2 * (ctx % 2)) * tokens, ctx * tokens), tokens)
        products(0, s_a, d_a, lower)

    both = pl.ds(pl.multiple_of(i * 2 * chunk, 2 * chunk), 2 * chunk)
    columns = pl.ds(first, 2 * chunk)

    def step(keys, next_keys):
        products(2 * i + 1, s_b, d_b, keys)
        qt_ref[:, columns] = qs[both, :].T
        weights(2 * i, 0, s_a, d_a, keys)
        products(jnp.minimum(2 * i + 2, chunks - 1), s_a, d_a, next_keys)
        dot_ref[:, columns] = dos[both, :].T
        weights(2 * i + 1, 1, s_b, d_b, keys)

    @pl.when(early)
    def _():
        step(lower, every)

    @pl.when(jnp.logical_not(early))
    def _():
        step(every, lower if blocks == 4 else every)


def far_kernel(
    sizes, start_ref, log1_ref, mean1_ref, qs_ref, dos_ref, qt_ref, dot_ref, *refs,
):
    tokens, groups, heads, slots, width, here, kept = sizes
    pair_refs = refs[:slots]
    k_ref, ds_ref, share_ref, shift_ref = refs[slots : slots + 4]
    part_refs = refs[slots + 4 : 2 * slots + 4]
    v_s, bias, dk, dv, s_a, d_a, s_b, d_b, w_s = refs[2 * slots + 4 :]
    chunk = here * groups
    blocks = tokens // here
    chunks = blocks * heads
    hops = slots // 2
    i = pl.program_id(0)
    first = step_rows(kept, 2 * chunk)
    slope = width**-0.5 * LOG2E
    ctx = lax.axis_index("ctx")
    reached = ctx >= 2
    steps = blocks // 2

    def products(c, s, d):
        rows = pl.ds(pl.multiple_of(c * chunk, chunk), chunk)
        h = c // blocks
        s[...] = lax.dot_general(qs_ref[rows, :], k_ref[h], ACROSS, preferred_element_type=f32)
        d[...] = lax.dot_general(dos_ref[rows, :], v_s[h], ACROSS, preferred_element_type=f32)

    def head_gradients(h):
        rows = slice(h * groups * tokens, (h + 1) * groups * tokens)
        grads = (
            jnp.dot(qt_ref[:, rows], ds_ref[rows, :], preferred_element_type=f32) * width**-0.5,
            jnp.dot(dot_ref[:, rows], w_s[rows, :], preferred_element_type=f32),
        )
        for source, grad in enumerate(grads):
            for slot, part in enumerate(part_refs):
                part[source, h * tokens : (h + 1) * tokens, :] = grad[
                    :, slot * tokens : (slot + 1) * tokens
                ].T.astype(bf16)

    def step_gradients():
        h = i // steps
        rows = pl.ds(pl.multiple_of(i * 2 * chunk, 2 * chunk), 2 * chunk)
        dk[h] += jnp.dot(qt_ref[:, rows], ds_ref[...], preferred_element_type=f32)
        dv[h] += jnp.dot(dot_ref[:, rows], w_s[...], preferred_element_type=f32)

    def weights(c, half, s, d, first):
        size = chunk // (2 if kept else 3)
        band = bias[pl.ds(pl.multiple_of(c % blocks * here, here), here), :]
        band = jnp.concatenate([band] * (size // here), 0)
        for row in range(0, chunk, size):
            rows = slice(row, row + size)
            out = pl.ds(first + half * chunk + row, size)
            log1 = log1_ref[out, :]
            mean1 = mean1_ref[out, :]
            x = s[rows, :] * slope + band
            dp = d[rows, :]
            m = jnp.maximum(jnp.max(x, -1, keepdims=True), log1)
            p = jnp.exp2(x - spread(m, x.shape[1]))
            before = jnp.exp2(log1 - m)
            inverse = 1.0 / (jnp.sum(p, -1, keepdims=True) + before)
            mean = (jnp.sum(p * dp, -1, keepdims=True) + before * mean1) * inverse
            w = p * spread(inverse, x.shape[1])
            ds = (w * (dp - spread(mean, x.shape[1]))).astype(bf16)
            there = out if kept else pl.ds(half * chunk + row, size)
            w_s[there, :] = w.astype(bf16)
            ds_ref[out, :] = ds
            share_ref[out, :] = before * inverse
            shift_ref[out, :] = mean1 - mean

    @pl.when(reached & (i == 0))
    def _():
        split_heads(pair_refs, k_ref, v_s, tokens, heads)
        partner = ctx + 1 - 2 * (ctx % 2)
        starts = [(ctx - 2 * d) * tokens for d in range(1, hops + 1)]
        starts += [(partner - 2 * d) * tokens for d in range(1, hops + 1)]
        fill_bias(bias, start_ref, starts, tokens)
        if not kept:
            dk[...] = jnp.zeros_like(dk)
            dv[...] = jnp.zeros_like(dv)
        products(0, s_a, d_a)

    def step(i, first):
        products(2 * i + 1, s_b, d_b)
        weights(2 * i, 0, s_a, d_a, first)
        products(jnp.minimum(2 * i + 2, chunks - 1), s_a, d_a)
        weights(2 * i + 1, 1, s_b, d_b, first)

    if kept:
        ends = [steps * h for h in range(1, heads)]
        plain = reached
        for end in ends:
            plain &= i != end

        @pl.when(plain)
        def _():
            step(i, first)

        for h, end in enumerate(ends):

            @pl.when(reached & (i == end))
            def _():
                head_gradients(h)
                step(end, end * 2 * chunk)

        @pl.when(reached & (i == pl.num_programs(0) - 1))
        def _():
            head_gradients(heads - 1)
    else:

        @pl.when(reached)
        def _():
            step(i, first)
            step_gradients()

        @pl.when(reached & (i == pl.num_programs(0) - 1))
        def _():
            join_heads(dk, dv, part_refs, tokens, heads, width**-0.5)

    @pl.when(jnp.logical_not(reached))
    def _():
        these = pl.ds(first, 2 * chunk)
        ds_ref[these, :] = jnp.zeros((2 * chunk, ds_ref.shape[1]), bf16)
        share_ref[these, :] = jnp.ones((2 * chunk, 128), f32)
        shift_ref[these, :] = jnp.zeros((2 * chunk, 128), f32)

    @pl.when(jnp.logical_not(reached) & (i == 0))
    def _():
        k_ref[...] = jnp.zeros_like(k_ref)
        for part in part_refs:
            part[...] = jnp.zeros_like(part)


def ahead_kernel(k_ref, ds_ref, dq_ref):
    heads = k_ref.shape[0]
    each = ds_ref.shape[0] // heads
    for h in range(heads):
        rows = slice(h * each, h * each + (each if h < heads - 1 else each // 2))
        dq_ref[rows, :] = jnp.dot(ds_ref[rows, :], k_ref[h], preferred_element_type=f32)


def tail_kernel(
    sizes, k1_ref, k2_ref, share_ref, shift_ref, w1_ref, u1_ref, ds2_ref, *refs,
):
    tokens, groups, heads, width, here, kept = sizes
    qt_refs, dot_refs = refs[:heads], refs[heads : 2 * heads]
    ahead_ref = refs[2 * heads]
    dq_ref, own_ref, partner_ref, dk, dv, *scratch = refs[2 * heads + (1 if kept else 0) :]
    chunk = here * groups
    i = pl.program_id(0)
    scale = width**-0.5
    first = step_rows(kept, chunk)

    @pl.when(i == 0)
    def _():
        dk[...] = jnp.zeros_like(dk)
        dv[...] = jnp.zeros_like(dv)

    def rescaled(h, w_s, ds_s, keys):
        size = 64 if chunk % 64 == 0 else chunk
        for row in range(0, chunk, size):
            rows = pl.ds(first + row, size)
            w = w1_ref[h, rows, :keys].astype(f32)
            share = spread(share_ref[h, rows, :], w.shape[1])
            shift = spread(shift_ref[h, rows, :], w.shape[1])
            w_s[row : row + size, :keys] = (w * share).astype(bf16)
            ds_s[row : row + size, :keys] = (
                (u1_ref[h, rows, :keys].astype(f32) + w * shift) * share
            ).astype(bf16)

    def gradients(h, w_s, ds_s, keys):
        columns = pl.ds((h * tokens * groups if kept else 0) + first, chunk)
        ds = ds_s[:, :keys]
        dk[h, :, :keys] += jnp.dot(qt_refs[h][:, columns], ds, preferred_element_type=f32)
        dv[h, :, :keys] += jnp.dot(
            dot_refs[h][:, columns], w_s[:, :keys], preferred_element_type=f32
        )
        dq = jnp.dot(ds, k1_ref[h, :keys], preferred_element_type=f32)
        if kept and (h < heads - 1 or keys < 2 * tokens):
            dq += ahead_ref[pl.ds(h * groups * tokens + first, chunk), :]
        else:
            dq += jnp.dot(
                ds2_ref[h, pl.ds(first, chunk), :], k2_ref[h], preferred_element_type=f32
            )
        dq *= scale
        for g in range(groups):
            dq_ref[pl.ds(g * heads + h, here, stride=groups * heads), :] = dq[
                g * here : (g + 1) * here
            ]

    def step(keys):
        for h in range(heads):
            rescaled(h, scratch[2 * h], scratch[2 * h + 1], keys)
        for h in range(heads):
            gradients(h, scratch[2 * h], scratch[2 * h + 1], keys)

    half = pl.num_programs(0) // 2
    pl.when(i < half)(lambda: step(tokens + tokens // 2))
    pl.when(i >= half)(lambda: step(2 * tokens))

    @pl.when(i == pl.num_programs(0) - 1)
    def _():
        join_heads(dk, dv, (partner_ref, own_ref), tokens, heads, scale)


def pack(keys, values, heads):
    return pl.pallas_call(
        functools.partial(pack_kernel, heads),
        in_specs=[pl.BlockSpec(memory_space=pltpu.HBM)] * 2,
        out_specs=VMEM,
        out_shape=jax.ShapeDtypeStruct((2, *keys.shape), bf16),
        scratch_shapes=[
            pltpu.VMEM((2, *keys.shape), bf16),
            pltpu.VMEM((2, *keys.shape), f32),
            pltpu.SemaphoreType.DMA((2,)),
        ],
        compiler_params=params(True, 4),
        name="pack",
    )(keys, values)


def finish(own, crossed, arrived, heads):
    return pl.pallas_call(
        functools.partial(finish_kernel, heads),
        in_specs=[VMEM] * (3 + len(arrived)),
        out_specs=[VMEM] * 2,
        out_shape=[jax.ShapeDtypeStruct(own.shape[1:], f32)] * 2,
        compiler_params=params(True, 8),
        name="finish",
    )(own, *crossed, *arrived)


def whole(*shape):
    return pl.BlockSpec(shape, lambda i: (0,) * len(shape))


def stepped(kept, *shape):
    return VMEM if kept else pl.BlockSpec(shape, lambda i: (i, 0))


def across(kept, *shape):
    return VMEM if kept else pl.BlockSpec(shape, lambda i: (0, i))


def params(kept, megabytes=16):
    return pltpu.CompilerParams(vmem_limit_bytes=(megabytes if kept else 60) * 2**20)


def step_rows(kept, rows):
    if not kept:
        return 0
    return pl.multiple_of(pl.program_id(0) * rows, rows)


def prep(q, do, sizes):
    tokens, groups, heads, width, here, kept = sizes
    rows = tokens * groups * heads
    pieces = 4
    return pl.pallas_call(
        functools.partial(prep_kernel, sizes),
        in_specs=[pl.BlockSpec(memory_space=pltpu.HBM)] * 2,
        out_specs=[VMEM] * 2,
        out_shape=[jax.ShapeDtypeStruct((rows, width), bf16)] * 2,
        scratch_shapes=[
            pltpu.VMEM((2 * pieces, rows // pieces, width), f32),
            pltpu.VMEM((pieces, rows // pieces, width), bf16),
            pltpu.VMEM((pieces, rows // pieces, width), bf16),
            pltpu.SemaphoreType.DMA((pieces, 2)),
        ],
        compiler_params=params(kept, 12),
        name="prep",
    )(q, do)


def near(qs, dos, start, own, partner, sizes):
    tokens, groups, heads, width, here, kept = sizes
    chunk = here * groups
    rows = tokens * groups * heads
    keys = 2 * tokens
    return pl.pallas_call(
        functools.partial(near_kernel, sizes),
        grid=(rows // (2 * chunk),),
        in_specs=[VMEM] * 5,
        out_specs=[
            stepped(kept, 2 * chunk, keys),
            stepped(kept, 2 * chunk, keys),
            whole(heads, keys, width),
            stepped(kept, 2 * chunk, 128),
            stepped(kept, 2 * chunk, 128),
            across(kept, width, 2 * chunk),
            across(kept, width, 2 * chunk),
        ],
        out_shape=[
            jax.ShapeDtypeStruct((rows, keys), bf16),
            jax.ShapeDtypeStruct((rows, keys), bf16),
            jax.ShapeDtypeStruct((heads, keys, width), bf16),
            jax.ShapeDtypeStruct((rows, 128), f32),
            jax.ShapeDtypeStruct((rows, 128), f32),
            jax.ShapeDtypeStruct((width, rows), bf16),
            jax.ShapeDtypeStruct((width, rows), bf16),
        ],
        scratch_shapes=[
            pltpu.VMEM((heads, keys, width), bf16),
            pltpu.VMEM((tokens, keys), f32),
        ]
        + [pltpu.VMEM((chunk, keys), f32)] * 4,
        compiler_params=params(kept, 12),
        cost_estimate=pl.CostEstimate(
            flops=2 * 2 * rows * (keys) * width,
            bytes_accessed=8 * rows * (keys),
            transcendentals=rows * (keys),
        ),
        name="near",
    )(qs, dos, start, own, partner)


def far(start, log1, mean1, qs, dos, qt, dt, pairs, sizes):
    tokens, groups, heads, width, here, kept = sizes
    slots = len(pairs)
    chunk = here * groups
    rows = tokens * groups * heads
    keys = slots * tokens
    return pl.pallas_call(
        functools.partial(far_kernel, (tokens, groups, heads, slots, width, here, kept)),
        grid=(rows // (2 * chunk),),
        in_specs=[VMEM] + [stepped(kept, 2 * chunk, 128)] * 2 + [VMEM] * (4 + slots),
        out_specs=[
            whole(heads, keys, width),
            stepped(kept, 2 * chunk, keys),
            stepped(kept, 2 * chunk, 128),
            stepped(kept, 2 * chunk, 128),
        ]
        + [whole(2, tokens * heads, width)] * slots,
        out_shape=[
            jax.ShapeDtypeStruct((heads, keys, width), bf16),
            jax.ShapeDtypeStruct((rows, keys), bf16),
            jax.ShapeDtypeStruct((rows, 128), f32),
            jax.ShapeDtypeStruct((rows, 128), f32),
        ]
        + [jax.ShapeDtypeStruct((2, tokens * heads, width), bf16)] * slots,
        scratch_shapes=[
            pltpu.VMEM((heads, keys, width), bf16),
            pltpu.VMEM((tokens, keys), f32),
            pltpu.VMEM((heads, width, keys), f32),
            pltpu.VMEM((heads, width, keys), f32),
        ]
        + [pltpu.VMEM((chunk, keys), f32)] * 4
        + [pltpu.VMEM((rows if kept else 2 * chunk, keys), bf16)],
        compiler_params=params(kept, 16),
        cost_estimate=pl.CostEstimate(
            flops=2 * 4 * rows * (keys) * width,
            bytes_accessed=8 * rows * (keys),
            transcendentals=rows * (keys),
        ),
        input_output_aliases={1: 2, 2: 3},
        name="far",
    )(start, log1, mean1, qs, dos, qt, dt, *pairs)


def ahead(k2, ds2):
    heads, _, width = k2.shape
    return pl.pallas_call(
        ahead_kernel,
        in_specs=[VMEM] * 2,
        out_specs=VMEM,
        out_shape=jax.ShapeDtypeStruct((ds2.shape[0] - ds2.shape[0] // (2 * heads), width), f32),
        compiler_params=params(True, 4),
        name="ahead",
    )(k2, ds2)


def tail(share, shift, k1, k2, qt, dt, w1, u1, ds2, early, sizes):
    tokens, groups, heads, width, here, kept = sizes
    chunk = here * groups
    rows = tokens * groups * heads
    blocks = tokens // here
    near_keys, far_keys = k1.shape[1], k2.shape[1]

    def both(columns):
        if kept:
            return VMEM
        return pl.BlockSpec((heads, chunk, columns), lambda i: (0, i, 0))

    def turned(h):
        if kept:
            return VMEM
        return pl.BlockSpec((width, chunk), lambda i: (0, h * blocks + i))

    def by_head(a):
        return a.reshape(heads, rows // heads, a.shape[1])

    return pl.pallas_call(
        functools.partial(tail_kernel, sizes),
        grid=(blocks,),
        in_specs=[
            whole(heads, near_keys, width),
            whole(heads, far_keys, width),
            both(128),
            both(128),
            both(near_keys),
            both(near_keys),
            both(far_keys),
        ]
        + [turned(h) for h in range(heads)] * 2
        + [VMEM] * len(early),
        out_specs=[pl.BlockSpec((chunk * heads, width), lambda i: (i, 0)), VMEM, VMEM],
        out_shape=[
            jax.ShapeDtypeStruct((rows, width), f32),
            jax.ShapeDtypeStruct((2, tokens * heads, width), f32),
            jax.ShapeDtypeStruct((2, tokens * heads, width), bf16),
        ],
        scratch_shapes=[
            pltpu.VMEM((heads, width, near_keys), f32),
            pltpu.VMEM((heads, width, near_keys), f32),
            *[pltpu.VMEM((chunk, near_keys), bf16)] * (2 * heads),
        ],
        compiler_params=params(kept, 12),
        cost_estimate=pl.CostEstimate(
            flops=6 * rows * (near_keys + far_keys) * width,
            bytes_accessed=8 * rows * (near_keys + far_keys),
            transcendentals=rows * (near_keys + far_keys),
        ),
        name="tail",
    )(
        k1,
        k2,
        *[by_head(a) for a in (share, shift, w1, u1, ds2)],
        *[qt] * heads,
        *[dt] * heads,
        *early,
    )


def shards(queries, keys, values, output_gradient, band_start):
    tokens, heads, groups, width = queries.shape
    count = lax.axis_size("ctx")
    reach = min(WINDOW // tokens, count - 1)
    hops = min((reach + 1) // 2, count // 2 - 1)

    def in_hbm(a):
        return pltpu.with_memory_space_constraint(a, pltpu.HBM)

    own = pack(
        in_hbm(keys.reshape(tokens * heads, width)),
        in_hbm(values.reshape(tokens * heads, width)),
        heads,
    )
    same = [moved(own, 2 * d) for d in range(1, hops + 1)]
    partner = swapped(own)
    start = band_start.reshape(1, tokens)
    kept = hops <= 2
    here = tokens // (4 if kept else 8)
    sizes = (tokens, groups, heads, width, here, kept)

    def flat(a):
        return a.transpose(0, 2, 1, 3).reshape(tokens * groups * heads, width)

    qs, dos = prep(in_hbm(flat(queries)), in_hbm(flat(output_gradient)), sizes)
    w1, u1, k1, log1, mean1, qt, dt = near(qs, dos, start, own, partner, sizes)
    *same, log1 = lax.optimization_barrier((*same, log1))
    other = [swapped(block) for block in same]
    k2, ds2, share, shift, *parts = far(
        start, log1, mean1, qs, dos, qt, dt, same + other, sizes
    )
    early = [ahead(k2, ds2)] if kept else []
    arriving = []
    for d in range(hops):
        crossed = swapped(parts[hops + d])
        both = (parts[d].astype(f32) + crossed.astype(f32)).astype(bf16)
        both, share, early = lax.optimization_barrier((both, share, early))
        arriving.append(moved(both, -2 * (d + 1)))
    dq, total, crossing = tail(
        share, shift, k1, k2, qt, dt, w1, u1, ds2, early, sizes
    )
    crossed = [swapped(half) for half in crossing]
    dk, dv = finish(total, crossed, arriving, heads)
    return (
        dq.reshape(tokens, groups, heads, width).transpose(0, 2, 1, 3),
        dk.reshape(tokens, heads, width),
        dv.reshape(tokens, heads, width),
    )


def solution(mesh):
    rows = P(("rep", "ctx"), "kv", None, None)
    keys = P(("rep", "ctx"), "kv", None)
    return jax.shard_map(
        shards,
        mesh=mesh,
        in_specs=(rows, keys, keys, rows, P(("rep", "ctx"))),
        out_specs=(rows, keys, keys),
        check_vma=False,
    )
```
